256 devices in a mesh: freq: 4 (over z_lo), slab: 16 (over y, x), xy: 4 (over z_hi, core).
Axes of the slice: x: 4, y: 4, z: 8 (z_hi: 2, z_lo: 4; z = z_hi * 4 + z_lo), core: 2. Of those that a mesh axis runs over, the one named last changes fastest.
Arguments:
- previous_field: float32 [2, 64, 128, 512], P(None, 'xy', 'slab', 'freq'), may hold values from -6 to 6
- current_field: float32 [2, 64, 128, 512], P(None, 'xy', 'slab', 'freq'), may hold values from -6 to 6
- courant: float32 [64, 128, 512], P('xy', 'slab', 'freq'), may hold values from 0.05 to 0.3
- wavelet: float32 [16], replicated, may hold values from -16 to 16
- traces: float32 [16, 256], replicated, may hold values from -12 to 12
- source_cell: int32 [1], replicated, may hold values from 0 to 4194303
- receiver_cells: int32 [256], replicated, may hold values from 0 to 4194303
- frequency_list: int32 [32], replicated, may hold values from 1 to 255
- lag_list: int32 [17], replicated, may hold values from -16 to 16, as said below
- spectra: float32 [2, 32, 2, 4, 16, 128, 512], P(None, 'freq', None, 'xy', 'slab'), may hold values from -24 to 24
Outputs:
- image: bfloat16 [17, 4, 16, 128, 512], P(None, 'xy', 'slab', 'freq')
The draws below stay inside these ranges and needn't reach their ends.
Inputs may be any that keep to these rules, and one draw needn't show every extreme that they name: `lag_list`: the list holds both -16 and 16. `receiver_cells`: receivers may share a cell.
All inputs are finite; a program needn't handle non-finite values.
Results may differ from the reference program's by a relative error of at most 0.02.
Values may be sent and summed in bfloat16 or wider, within the bound.
A program may use at most 128 MiB of HBM per device.

```python
import math
import jax
import jax.numpy as jnp
from jax import lax

CZ = 16
NREC = 256
STEPS = 16
NTOT = 2048
FREQ_DEV = 8
LAGS = 17
LAGMAX = 16
NZ = 64
NY = 128
NX = 512
NFREQ = 32
N_FREQ = 4
N_XY = 4


def draw_lag_list(key, part):
    key = jax.random.fold_in(key, 7)
    first_key, second_key = jax.random.split(key)
    inner = jax.random.randint(first_key, (LAGS - 2,), -LAGMAX, LAGMAX + 1, dtype=jnp.int32)
    values = jnp.concatenate([jnp.array([-LAGMAX, LAGMAX], jnp.int32), inner])
    return values[jax.random.permutation(second_key, LAGS)]


def set_ends(result, rng, low, top_value):
    index_at = [jax.random.randint(jax.random.fold_in(rng, axis), (), 0, length) for axis, length in enumerate(result.shape)]
    longest = result.shape.index(max(result.shape))
    beside = index_at[:longest] + [(index_at[longest] + 1) % result.shape[longest]] + index_at[longest + 1:]
    return result.at[tuple(index_at)].set(low).at[tuple(beside)].set(top_value)


def level_of(rng, shape, cuts, low, high):
    level, own = 1.0, jax.random.fold_in(rng, 6)
    for dim, shards_of in cuts:
        draws = jnp.exp(jax.random.uniform(jax.random.fold_in(own, dim), (shards_of,), jnp.float32, low / len(cuts), high / len(cuts)))
        level = level * jnp.repeat(draws, shape[dim] // shards_of).reshape([-1 if axis == dim else 1 for axis in range(len(shape))])
    return level


def noise(key, extent, scale, most, cuts=(), held_as=jnp.bfloat16):
    drawn = scale * jax.random.normal(key, extent, jnp.float32)
    if cuts:
        drawn = drawn * level_of(key, extent, cuts, -0.22, 0.18)
    return jnp.clip(drawn, -most, most).astype(held_as)


def setup_inputs(seed: int = 0) -> dict:
    keys = jax.random.split(jax.random.key(seed), 11)
    previous_field = noise(keys[0], (2, NZ, NY, NX), 1.0, 6.0, ((1, 4), (2, 16), (3, 4)), jnp.float32)
    current_field = noise(keys[1], (2, NZ, NY, NX), 1.0, 6.0, ((1, 4), (2, 16), (3, 4)), jnp.float32)
    courant = jnp.clip(jnp.exp(math.log(0.3) - 1.7917595 * jax.random.uniform(keys[2], (NZ, NY, NX), jnp.float32) ** level_of(keys[2], (NZ, NY, NX), ((0, 4), (1, 16), (2, 4)), -0.2, 0.2)), 0.05, 0.3)
    wavelet = noise(keys[3], (STEPS,), 4.0, 16.0, (), jnp.float32)
    traces = noise(keys[4], (STEPS, NREC), 2.0, 12.0, (), jnp.float32)
    source_cell = jax.random.randint(keys[5], (1,), 0, NZ * NY * NX).astype(jnp.int32)
    receiver_cells = set_ends(jax.random.randint(keys[6], (NREC,), 0, NZ * NY * NX), jax.random.fold_in(keys[6], 1), 0, (NZ * NY * NX) - 1).astype(jnp.int32)
    frequency_list = set_ends(jax.random.randint(keys[7], (NFREQ,), 1, NTOT // 8), jax.random.fold_in(keys[7], 1), 1, (NTOT // 8) - 1).astype(jnp.int32)
    lag_list = draw_lag_list(jax.random.fold_in(keys[10], 71), 0)
    spectra = noise(keys[9], (2, NFREQ, 2, N_XY, CZ, NY, NX), 4.0, 24.0, ((1, 4), (3, 4), (4, 16)), jnp.float32)
    return {"previous_field": previous_field, "current_field": current_field, "courant": courant, "wavelet": wavelet, "traces": traces, "source_cell": source_cell, "receiver_cells": receiver_cells, "frequency_list": frequency_list, "lag_list": lag_list, "spectra": spectra}


def dft_table(frequency_list):
    moments = jnp.arange(STEPS, dtype=jnp.int32) + (NTOT - STEPS)
    phase_index = (moments[:, None] * frequency_list[None, :].astype(jnp.int32)) % NTOT
    phase_angle = phase_index.astype(jnp.float32) * (2.0 * math.pi / NTOT)
    return jnp.stack([jnp.cos(phase_angle), -jnp.sin(phase_angle)], axis=-1).astype(jnp.bfloat16)


def step_field(previous, current, courant, injection):
    padded = jnp.pad(current, ((0, 0), (1, 1), (1, 1), (1, 1)))
    beside = padded[:, 2:, 1:-1, 1:-1] + padded[:, :-2, 1:-1, 1:-1]
    beside = beside + padded[:, 1:-1, 2:, 1:-1] + padded[:, 1:-1, :-2, 1:-1]
    beside = beside + padded[:, 1:-1, 1:-1, 2:] + padded[:, 1:-1, 1:-1, :-2]
    return 2.0 * current - previous + courant * (beside - 6.0 * current) + injection


def reference(previous_field, current_field, courant, wavelet, traces, source_cell, receiver_cells, frequency_list, lag_list, spectra):
    cell_total = NZ * NY * NX

    def advance(state, moment):
        previous, current = state
        injection = jnp.zeros((2, cell_total), jnp.float32)
        injection = injection.at[0, source_cell].add(wavelet[moment])
        injection = injection.at[1, receiver_cells].add(traces[moment])
        following = step_field(previous, current, courant, injection.reshape(current.shape))
        return (current, following), following.astype(jnp.bfloat16)

    end_state, snapshots = lax.scan(advance, (previous_field, current_field), jnp.arange(STEPS, dtype=jnp.int32))
    dft_rows = dft_table(frequency_list).astype(jnp.float32)
    flat_snap = snapshots.reshape(STEPS, 2, cell_total)
    prior_spec = spectra.reshape(2, NFREQ, 2, cell_total)
    fresh_spec = [prior_spec[field_id] + jnp.einsum("tkp,tc->kpc", dft_rows, flat_snap[:, field_id].astype(jnp.float32)) for field_id in range(2)]
    term_count = NFREQ * 2
    group_terms = FREQ_DEV * 2
    widths = ((0, 0), (0, 0), (0, 0), (LAGMAX, LAGMAX))
    padded_source = jnp.pad(fresh_spec[0].reshape(term_count, NZ, NY, NX), widths)
    padded_receiver = jnp.pad(fresh_spec[1].reshape(term_count, NZ, NY, NX), widths)
    weight = 1.0 / (STEPS * NFREQ)
    zero_start = jnp.int32(0)

    def one_lag(offset_value):
        offset_value = offset_value.astype(jnp.int32)

        def add_term(term_index, running):
            term_index = jnp.asarray(term_index).astype(jnp.int32)
            early_terms = lax.dynamic_slice(padded_source, (term_index, zero_start, zero_start, (LAGMAX - offset_value).astype(jnp.int32)), (1, NZ, NY, NX))[0]
            late_terms = lax.dynamic_slice(padded_receiver, (term_index, zero_start, zero_start, (LAGMAX + offset_value).astype(jnp.int32)), (1, NZ, NY, NX))[0]
            return running + early_terms * late_terms

        summed_image = jnp.zeros((NZ, NY, NX), jnp.float32)
        for group_id in range(N_FREQ):
            group_sum = lax.fori_loop(group_id * group_terms, (group_id + 1) * group_terms, add_term, jnp.zeros((NZ, NY, NX), jnp.float32))
            rounded = lax.optimization_barrier((group_sum * weight).astype(jnp.bfloat16))
            summed_image = summed_image + rounded.astype(jnp.float32)
        return summed_image.astype(jnp.bfloat16)

    image = lax.map(one_lag, lag_list)
    return image.reshape(LAGS, N_XY, CZ, NY, NX)
```

```python
import functools
import math

import jax
import jax.numpy as jnp
from jax import lax
from jax.experimental import pallas as pl
from jax.experimental.pallas import tpu as pltpu
from jax.sharding import PartitionSpec as P

STEPS = 16
NTOT = 2048
LAGMAX = 16
NF, NS, NB = 4, 16, 4
ROWS, COLS = 32, 512
TERMS = 16
NY = NF * ROWS
F32, BF16 = jnp.float32, jnp.bfloat16
MESH = pl.DeviceIdType.MESH


def dft_table(frequency_list):
    moments = jnp.arange(STEPS, dtype=jnp.int32) + (NTOT - STEPS)
    phase_index = moments[:, None] * frequency_list[None, :] % NTOT
    phase_angle = phase_index.astype(F32) * (2.0 * math.pi / NTOT)
    return jnp.stack([jnp.cos(phase_angle), -jnp.sin(phase_angle)], axis=-1).astype(BF16)


def window_kernel(
    prev_ref, cur_ref, cour_ref, wav_ref, traces_ref, src_ref, rec_ref, spec_ref,
    planes, fresh,
    raw, outgoing, pieces_out, pieces_in, field, cour, inj, lo, hi, yout, yin,
    raw_sem, spec_send, spec_recv, piece_send, piece_recv,
    zsend, zrecv, ysend, yrecv,
):
    f, j, b = lax.axis_index("freq"), lax.axis_index("slab"), lax.axis_index("xy")
    z = b * NS + j
    has_lo, has_hi = z > 0, z < NB * NS - 1
    has_top, has_bottom = f > 0, f < NF - 1

    def plane_at(depth):
        return {"freq": f, "slab": depth % NS, "xy": depth // NS}

    def group_at(other):
        return {"freq": other, "slab": j, "xy": b}

    peers = (lax.rem(f + 2, NF), NF - 1 - f, f + 1 - 2 * lax.rem(f, 2))
    chunk = (f,) + peers

    def raw_copy(o, w):
        return pltpu.make_async_copy(
            spec_ref.at[w, :, pl.ds(chunk[o] * ROWS, ROWS), :], raw.at[o, w], raw_sem.at[o, w]
        )

    for o in (1, 2, 3, 0):
        for w in range(2):
            raw_copy(o, w).start()

    barrier = pltpu.get_barrier_semaphore()
    target_f = j // 4
    mine = target_f == f

    for p in peers:
        pl.semaphore_signal(barrier, 1, device_id=group_at(p), device_id_type=MESH)

    @pl.when(has_lo)
    def _():
        pl.semaphore_signal(barrier, 1, device_id=plane_at(z - 1), device_id_type=MESH)

    @pl.when(has_hi)
    def _():
        pl.semaphore_signal(barrier, 1, device_id=plane_at(z + 1), device_id_type=MESH)

    def greet(i, carry):
        f0, j0 = i // 4, 4 * f + i % 4

        @pl.when(jnp.logical_not((f0 == f) & (j0 == j)))
        def _():
            pl.semaphore_signal(
                barrier, 1, device_id={"freq": f0, "slab": j0, "xy": b}, device_id_type=MESH
            )

        return carry

    lax.fori_loop(0, 16, greet, 0)

    def stack(i, carry):
        for w in range(2):
            pieces_out[i, w] = prev_ref[w, i]
            pieces_out[i, 2 + w] = cur_ref[w, i]
        pieces_out[i, 4] = cour_ref[i]
        return carry

    lax.fori_loop(0, NS, stack, 0)

    expected = len(peers) + NS + has_lo.astype(jnp.int32) + has_hi.astype(jnp.int32)
    pl.semaphore_wait(barrier, expected - mine.astype(jnp.int32))

    place = f * 4 + j % 4

    def piece_copy(i):
        return pltpu.make_async_remote_copy(
            src_ref=pieces_out.at[i],
            dst_ref=pieces_in.at[place],
            send_sem=piece_send.at[i],
            recv_sem=piece_recv.at[place],
            device_id={"freq": target_f, "slab": i, "xy": b},
            device_id_type=MESH,
        )

    def is_self(i):
        return mine & (i == j)

    def send_piece(i, carry):
        @pl.when(jnp.logical_not(is_self(i)))
        def _():
            piece_copy(i).start()

        return carry

    lax.fori_loop(0, NS, send_piece, 0)

    @pl.when(mine)
    def _():
        pieces_in[place] = pieces_out[j]

    def spec_copy(o, w):
        return pltpu.make_async_remote_copy(
            src_ref=outgoing.at[o - 1, w],
            dst_ref=fresh.at[f, w],
            send_sem=spec_send.at[o - 1, w],
            recv_sem=spec_recv.at[f, w],
            device_id=group_at(chunk[o]),
            device_id_type=MESH,
        )

    for o in (1, 2, 3):
        for w in range(2):
            raw_copy(o, w).wait()

            def cast(i, carry, o=o, w=w):
                outgoing[o - 1, w, i] = raw[o, w, i].astype(BF16)
                return carry

            lax.fori_loop(0, TERMS, cast, 0)
            spec_copy(o, w).start()

    cell = rec_ref[...]
    depth, row, col = cell >> 16, (cell >> 9) & (NY - 1), cell & (COLS - 1)
    row = jnp.where(depth == z, row - f * ROWS, -1)
    at_row = lax.broadcasted_iota(jnp.int32, (ROWS, cell.shape[1]), 0) == row
    at_col = (lax.broadcasted_iota(jnp.int32, (COLS, cell.shape[1]), 0) == col).astype(F32).astype(BF16)

    def inject(t, carry):
        values = jnp.where(at_row, traces_ref[pl.ds(t, 1), :], 0.0)
        first = values.astype(BF16)
        rest = values - first.astype(F32)
        second = rest.astype(BF16)
        third = (rest - second.astype(F32)).astype(BF16)
        parts = lax.dot_general(
            jnp.concatenate([first, second, third], axis=0), at_col,
            (((1,), (1,)), ((), ())), preferred_element_type=F32,
        )
        inj[t] = parts[:ROWS] + parts[ROWS : 2 * ROWS] + parts[2 * ROWS :]
        return carry

    lax.fori_loop(0, STEPS, inject, 0)

    row_id = lax.broadcasted_iota(jnp.int32, (ROWS, COLS), 0)
    col_id = lax.broadcasted_iota(jnp.int32, (ROWS, COLS), 1)

    for i in range(16):
        f0, jj = i // 4, i % 4

        @pl.when(jnp.logical_not((f == f0) & (j == 4 * f + jj)))
        def _(i=i):
            pltpu.make_async_remote_copy(
                src_ref=pieces_out.at[0], dst_ref=pieces_in.at[i],
                send_sem=piece_send.at[0], recv_sem=piece_recv.at[i],
                device_id=group_at(f), device_id_type=MESH,
            ).wait_recv()

        rows, cols = pl.ds(8 * jj, 8), pl.ds(128 * f0, 128)
        for w in range(2):
            field[1, w, rows, cols] = pieces_in[i, w]
            field[0, w, rows, cols] = pieces_in[i, 2 + w]
        cour[rows, cols] = pieces_in[i, 4]

    def z_copy(s, up):
        return pltpu.make_async_remote_copy(
            src_ref=planes.at[s],
            dst_ref=(lo if up else hi).at[s],
            send_sem=zsend.at[s, int(up)],
            recv_sem=zrecv.at[s, int(up)],
            device_id=plane_at(z + 1 if up else z - 1),
            device_id_type=MESH,
        )

    def y_copy(s, down):
        return pltpu.make_async_remote_copy(
            src_ref=yout.at[s, int(down)],
            dst_ref=yin.at[s, int(down)],
            send_sem=ysend.at[s, int(down)],
            recv_sem=yrecv.at[s, int(down)],
            device_id=group_at(f + 1 if down else f - 1),
            device_id_type=MESH,
        )

    def publish(s, values):
        for w in range(2):
            planes[s, w] = values[w].astype(BF16)

    def send(s, values):
        for w in range(2):
            for i in range(4):
                cols = slice(128 * i, 128 * (i + 1))
                yout[s, 0, pl.ds(4 * w + i, 1), :] = values[w][0:1, cols]
                yout[s, 1, pl.ds(4 * w + i, 1), :] = values[w][ROWS - 1 : ROWS, cols]

        @pl.when(has_hi)
        def _():
            z_copy(s, True).start()

        @pl.when(has_lo)
        def _():
            z_copy(s, False).start()

        @pl.when(has_bottom)
        def _():
            y_copy(s, True).start()

        @pl.when(has_top)
        def _():
            y_copy(s, False).start()

    first = [field[0, w] for w in range(2)]
    publish(0, first)
    send(0, first)

    source = src_ref[0]
    source_row = jnp.where((source >> 16) == z, ((source >> 9) & (NY - 1)) - f * ROWS, -1)
    at_source = (row_id == source_row) & (col_id == (source & (COLS - 1)))

    def arrivals(s, present, copy, there):
        @pl.when(present)
        def _():
            copy.wait_recv()

        @pl.when(jnp.logical_not(present))
        def _():
            there[s] = jnp.zeros(there.shape[1:], there.dtype)

    def advance(t, carry):
        now, other = t % 2, (t + 1) % 2
        arrivals(t, has_lo, z_copy(t, True), lo)
        arrivals(t, has_hi, z_copy(t, False), hi)
        arrivals(t, has_top, y_copy(t, True), yin.at[:, 1])
        arrivals(t, has_bottom, y_copy(t, False), yin.at[:, 0])
        values = []
        for w in range(2):
            u = field[now, w]
            top = jnp.concatenate([yin[t, 1, pl.ds(4 * w + i, 1), :] for i in range(4)], axis=1)
            bottom = jnp.concatenate([yin[t, 0, pl.ds(4 * w + i, 1), :] for i in range(4)], axis=1)
            beside = lo[t, w].astype(F32) + hi[t, w].astype(F32)
            beside += jnp.where(row_id == 0, top, pltpu.roll(u, 1, 0))
            beside += jnp.where(row_id == ROWS - 1, bottom, pltpu.roll(u, ROWS - 1, 0))
            beside += jnp.where(col_id == 0, 0.0, pltpu.roll(u, 1, 1))
            beside += jnp.where(col_id == COLS - 1, 0.0, pltpu.roll(u, COLS - 1, 1))
            injection = inj[t] if w == 1 else jnp.where(at_source, wav_ref[t], 0.0)
            following = 2.0 * u - field[other, w] + cour[...] * (beside - 6.0 * u) + injection
            field[other, w] = following
            values.append(following)
        publish(t + 1, values)

        @pl.when(t < STEPS - 1)
        def _():
            send(t + 1, values)

        return carry

    lax.fori_loop(0, STEPS, advance, 0)

    for w in range(2):
        raw_copy(0, w).wait()

        def cast_own(i, carry, w=w):
            fresh[f, w, i] = raw[0, w, i].astype(BF16)
            return carry

        lax.fori_loop(0, TERMS, cast_own, 0)

    def sent(s, carry):
        @pl.when(has_hi)
        def _():
            z_copy(s, True).wait_send()

        @pl.when(has_lo)
        def _():
            z_copy(s, False).wait_send()

        @pl.when(has_bottom)
        def _():
            y_copy(s, True).wait_send()

        @pl.when(has_top)
        def _():
            y_copy(s, False).wait_send()

        @pl.when(jnp.logical_not(is_self(s)))
        def _():
            piece_copy(s).wait_send()

        return carry

    lax.fori_loop(0, STEPS, sent, 0)

    for o in (1, 2, 3):
        for w in range(2):
            spec_copy(o, w).wait_send()
            pltpu.make_async_remote_copy(
                src_ref=outgoing.at[o - 1, w], dst_ref=fresh.at[chunk[o], w],
                send_sem=spec_send.at[o - 1, w], recv_sem=spec_recv.at[chunk[o], w],
                device_id=group_at(chunk[o]), device_id_type=MESH,
            ).wait_recv()


def window(previous_field, current_field, courant, wavelet, traces, source_cell, receiver_cells, spectra):
    vmem = pl.BlockSpec(memory_space=pltpu.VMEM)
    smem = pl.BlockSpec(memory_space=pltpu.SMEM)
    dma = pltpu.SemaphoreType.DMA
    plane = (2, ROWS, COLS)
    return pl.pallas_call(
        window_kernel,
        out_shape=(
            jax.ShapeDtypeStruct((STEPS + 1,) + plane, BF16),
            jax.ShapeDtypeStruct((NF, 2, TERMS, ROWS, COLS), BF16),
        ),
        in_specs=[vmem, vmem, vmem, smem, vmem, smem, vmem, pl.BlockSpec(memory_space=pl.ANY)],
        out_specs=(vmem, vmem),
        scratch_shapes=[
            pltpu.VMEM((NF, 2, TERMS, ROWS, COLS), F32),
            pltpu.VMEM((NF - 1, 2, TERMS, ROWS, COLS), BF16),
            pltpu.VMEM((NS, 5, 8, 128), F32),
            pltpu.VMEM((16, 5, 8, 128), F32),
            pltpu.VMEM((2,) + plane, F32),
            pltpu.VMEM((ROWS, COLS), F32),
            pltpu.VMEM((STEPS, ROWS, COLS), F32),
            pltpu.VMEM((STEPS,) + plane, BF16),
            pltpu.VMEM((STEPS,) + plane, BF16),
            pltpu.VMEM((STEPS, 2, 8, 128), F32),
            pltpu.VMEM((STEPS, 2, 8, 128), F32),
            dma((NF, 2)),
            dma((NF - 1, 2)),
            dma((NF, 2)),
            dma((NS,)),
            dma((16,)),
            dma((STEPS, 2)),
            dma((STEPS, 2)),
            dma((STEPS, 2)),
            dma((STEPS, 2)),
        ],
        compiler_params=pltpu.CompilerParams(
            collective_id=0, has_side_effects=True, vmem_limit_bytes=48 * 2**20
        ),
        name="window",
    )(
        previous_field, current_field, courant, wavelet, traces, source_cell,
        receiver_cells.reshape(1, -1), spectra,
    )


HALF = 16


def image_kernel(lag_ref, mix_ref, planes, fresh, out, early, late):
    lanes = lax.broadcasted_iota(jnp.int32, (HALF, 128), 1)
    columns = lax.broadcasted_iota(jnp.int32, (HALF, COLS), 1)
    terms = NF * TERMS
    weight = 1.0 / (STEPS * terms / 2)

    for half in range(ROWS // HALF):
        rows = pl.ds(half * HALF, HALF)
        for w, held in ((0, early), (1, late)):
            snaps = planes[pl.ds(1, STEPS), w, rows, :].reshape(STEPS * HALF, COLS)

            def gather(g, carry, w=w, held=held, snaps=snaps, rows=rows):
                part = jnp.dot(
                    mix_ref[pl.ds(pl.multiple_of(g * TERMS * HALF, TERMS * HALF), TERMS * HALF), :],
                    snaps, preferred_element_type=F32,
                )
                total = part.reshape(TERMS, HALF, COLS) + fresh[g, w, :, rows, :].astype(F32)
                if w == 1:
                    total = pltpu.roll(total, 2 * LAGMAX, 2)
                held[pl.ds(g * TERMS, TERMS)] = total
                return carry

            lax.fori_loop(0, NF, gather, 0)

        def one_lag(h, carry, rows=rows, half=half):
            lag = lag_ref[h]
            ahead = 2 * lag + 2 * LAGMAX
            back = lax.rem(128 - ahead, 128)
            inside = lanes < 128 - ahead

            def add(k, sums):
                for i in range(4):
                    term = k * 4 + i
                    turned = [
                        pltpu.roll(late[term, :, pl.ds(128 * c, 128)], back, 1) for c in range(4)
                    ]
                    sums = tuple(
                        sums[c]
                        + early[term, :, pl.ds(128 * c, 128)]
                        * jnp.where(inside, turned[c], turned[(c + 1) % 4])
                        for c in range(4)
                    )
                return sums

            sums = lax.fori_loop(
                0, terms // 4, add, tuple(jnp.zeros((HALF, 128), F32) for _ in range(4))
            )
            total = jnp.concatenate(sums, axis=1) * weight
            total = pltpu.roll(total, COLS - LAGMAX, 1)
            forward = lag + LAGMAX
            turned = [pltpu.roll(total[:, 128 * c : 128 * (c + 1)], forward, 1) for c in range(4)]
            moved = jnp.concatenate(
                [jnp.where(lanes < forward, turned[(c + 3) % 4], turned[c]) for c in range(4)], axis=1
            )
            reach = jnp.abs(lag)
            kept = jnp.where((columns >= reach) & (columns < COLS - reach), moved, 0.0)
            out[h, rows, :] = kept.astype(BF16)
            return carry

        lax.fori_loop(0, lag_ref.shape[0], one_lag, 0)


def make_image(lag_list, mix, planes, fresh):
    vmem = pl.BlockSpec(memory_space=pltpu.VMEM)
    lags = lag_list.shape[0]
    return pl.pallas_call(
        image_kernel,
        out_shape=jax.ShapeDtypeStruct((lags, ROWS, COLS), BF16),
        in_specs=[pl.BlockSpec(memory_space=pltpu.SMEM), vmem, vmem, vmem],
        out_specs=vmem,
        scratch_shapes=[
            pltpu.VMEM((NF * TERMS, HALF, COLS), F32),
            pltpu.VMEM((NF * TERMS, HALF, COLS), F32),
        ],
        compiler_params=pltpu.CompilerParams(vmem_limit_bytes=48 * 2**20),
        name="image",
    )(lag_list, mix, planes, fresh)


def body(
    previous_field, current_field, courant, wavelet, traces, source_cell, receiver_cells,
    frequency_list, lag_list, spectra,
):
    table = dft_table(frequency_list).reshape(STEPS, NF * TERMS)
    same = jnp.eye(HALF, dtype=BF16)
    mix = (table.T[:, None, :, None] * same[None, :, None, :]).reshape(NF * TERMS * HALF, STEPS * HALF)
    planes, fresh = window(
        previous_field, current_field, courant, wavelet, traces, source_cell, receiver_cells,
        spectra.reshape(2, TERMS, NY, COLS),
    )
    image = make_image(lag_list, mix, planes, fresh)
    return image.reshape(lag_list.shape[0], 1, 1, ROWS, COLS)


def solution(mesh):
    placed = (
        P(None, "xy", "slab", "freq"),
        P(None, "xy", "slab", "freq"),
        P("xy", "slab", "freq"),
        P(),
        P(),
        P(),
        P(),
        P(),
        P(),
        P(None, "freq", None, "xy", "slab", None, None),
    )
    return jax.shard_map(
        body,
        mesh=mesh,
        in_specs=placed,
        out_specs=P(None, "xy", "slab", "freq", None),
        check_vma=False,
    )
```

```python
import math

import jax
import jax.numpy as jnp
from jax import lax
from jax.experimental import pallas as pl
from jax.experimental.pallas import tpu as pltpu
from jax.sharding import PartitionSpec as P

STEPS = 16
NTOT = 2048
LAGMAX = 16
NF, NS, NB = 4, 16, 4
ROWS, COLS = 32, 512
DEEP, WIDE = 4, 8
TERMS = 16
NY = NF * ROWS
F32, BF16 = jnp.float32, jnp.bfloat16
XS = 128
BLOCKS = COLS // XS
HALF = 16
ROUND = 4
BESIDE = 10
MESH = pl.DeviceIdType.MESH


def dft_table(frequency_list):
    moments = jnp.arange(STEPS, dtype=jnp.int32) + (NTOT - STEPS)
    phase_index = moments[:, None] * frequency_list[None, :] % NTOT
    phase_angle = phase_index.astype(F32) * (2.0 * math.pi / NTOT)
    return jnp.stack([jnp.cos(phase_angle), -jnp.sin(phase_angle)], axis=-1).astype(BF16)


def turned(rows):
    return jnp.concatenate([rows[:, XS * c : XS * (c + 1)] for c in range(BLOCKS)], axis=0).T


def kernel(
    prev_ref, cur_ref, cour_ref, wav_ref, traces_ref, src_ref, rec_ref, lag_ref, table_ref, spec_ref,
    out,
    raw, outgoing, fresh, pieces_out, pieces_in, field, cour, inj, planes, held, lo, hi, yout, yin,
    spread, mix, snaps, early, late, sums,
    raw_sem, spec_send, spec_recv, piece_send, piece_recv,
    zsend, zrecv, ysend, yrecv, held_send, held_recv,
):
    f, j, b = lax.axis_index("freq"), lax.axis_index("slab"), lax.axis_index("xy")
    deep, wide = j // 4, j % 4
    layer, strip = b * 4 + deep, f * 4 + wide
    first_plane, first_row = layer * DEEP, strip * WIDE
    has_lo, has_hi = layer > 0, layer < NB * 4 - 1
    has_top, has_bottom = strip > 0, strip < NF * 4 - 1
    lags = lag_ref.shape[0]

    def layer_at(other):
        return {"freq": f, "slab": (other % 4) * 4 + wide, "xy": other // 4}

    def strip_at(other):
        return {"freq": other // 4, "slab": deep * 4 + other % 4, "xy": b}

    def group_at(other):
        return {"freq": other, "slab": j, "xy": b}

    def plane_at(other):
        return {"freq": f, "slab": deep * 4 + other, "xy": b}

    peers = (lax.rem(f + 2, NF), NF - 1 - f, f + 1 - 2 * lax.rem(f, 2))
    chunk = peers + (f,)
    mates = tuple(lax.rem(wide + n, 4) for n in (1, 2, 3))

    def raw_copy(o, w):
        return pltpu.make_async_copy(
            spec_ref.at[w, :, pl.ds(chunk[o] * ROWS, ROWS), :], raw.at[o, w], raw_sem.at[o, w]
        )

    for o in range(NF):
        for w in range(2):
            raw_copy(o, w).start()

    barrier = pltpu.get_barrier_semaphore()
    mine = deep == f

    def greet(there):
        pl.semaphore_signal(barrier, 1, device_id=there, device_id_type=MESH)

    for p in peers:
        greet(group_at(p))
    for m in mates:
        greet(plane_at(m))
    for present, there in (
        (has_lo, layer_at(layer - 1)), (has_hi, layer_at(layer + 1)),
        (has_top, strip_at(strip - 1)), (has_bottom, strip_at(strip + 1)),
    ):
        @pl.when(present)
        def _(there=there):
            greet(there)

    for f0 in range(NF):
        @pl.when(jnp.logical_not(mine & (f == f0)))
        def _(f0=f0):
            greet({"freq": f0, "slab": 4 * f + wide, "xy": b})

    def stack(i, carry):
        group, p = i // DEEP, i % DEEP
        for w in range(2):
            pieces_out[group, w, p] = prev_ref[w, i]
            pieces_out[group, 2 + w, p] = cur_ref[w, i]
        pieces_out[group, 4, p] = cour_ref[i]
        return carry

    lax.fori_loop(0, NS, stack, 0)

    expected = len(peers) + len(mates) + NF - mine.astype(jnp.int32)
    for present in (has_lo, has_hi, has_top, has_bottom):
        expected += present.astype(jnp.int32)
    pl.semaphore_wait(barrier, expected)

    def piece_copy(group):
        return pltpu.make_async_remote_copy(
            src_ref=pieces_out.at[group],
            dst_ref=pieces_in.at[f],
            send_sem=piece_send.at[group],
            recv_sem=piece_recv.at[f],
            device_id={"freq": deep, "slab": 4 * group + wide, "xy": b},
            device_id_type=MESH,
        )

    for group in range(4):
        @pl.when(jnp.logical_not(mine & (deep == group)))
        def _(group=group):
            piece_copy(group).start()

    @pl.when(mine)
    def _():
        pieces_in[f] = pieces_out[deep]

    cell = rec_ref[...]
    depth, row, col = (cell >> 16) - first_plane, ((cell >> 9) & (NY - 1)) - first_row, cell & (COLS - 1)
    here = (depth >= 0) & (depth < DEEP) & (row >= 0) & (row < WIDE)
    row = jnp.where(here, depth * WIDE + row, -1)
    at_row = lax.broadcasted_iota(jnp.int32, (ROWS, cell.shape[1]), 0) == row
    at_col = (lax.broadcasted_iota(jnp.int32, (COLS, cell.shape[1]), 0) == col).astype(F32).astype(BF16)

    def inject(t, carry):
        values = jnp.where(at_row, traces_ref[pl.ds(t, 1), :], 0.0)
        first = values.astype(BF16)
        rest = values - first.astype(F32)
        second = rest.astype(BF16)
        third = (rest - second.astype(F32)).astype(BF16)
        parts = lax.dot_general(
            jnp.concatenate([first, second, third], axis=0), at_col,
            (((1,), (1,)), ((), ())), preferred_element_type=F32,
        )
        inj[t] = (parts[:ROWS] + parts[ROWS : 2 * ROWS] + parts[2 * ROWS :]).reshape(DEEP, WIDE, COLS)
        return carry

    lax.fori_loop(0, STEPS, inject, 0)

    terms = NF * TERMS
    step_of = lax.broadcasted_iota(jnp.int32, (STEPS, STEPS * HALF), 1) // HALF
    chosen = (step_of == lax.broadcasted_iota(jnp.int32, (STEPS, STEPS * HALF), 0)).astype(F32).astype(BF16)
    spread[...] = jnp.dot(table_ref[...], chosen, preferred_element_type=F32)
    place = lax.broadcasted_iota(jnp.int32, (HALF, STEPS * HALF), 1) % HALF
    diagonal = place == lax.broadcasted_iota(jnp.int32, (HALF, STEPS * HALF), 0)

    def fill(k, carry):
        values = jnp.where(diagonal, spread[pl.ds(k, 1), :], 0.0)
        mix[pl.ds(pl.multiple_of(k * HALF, HALF), HALF), :] = values.astype(BF16)
        return carry

    lax.fori_loop(0, terms, fill, 0)

    for o in range(NF):
        for w in range(2):
            raw_copy(o, w).wait()

    row_id = lax.broadcasted_iota(jnp.int32, (WIDE, COLS), 0)
    col_id = lax.broadcasted_iota(jnp.int32, (WIDE, COLS), 1)

    for f0 in range(NF):
        @pl.when(jnp.logical_not(mine & (f == f0)))
        def _(f0=f0):
            pltpu.make_async_remote_copy(
                src_ref=pieces_out.at[0], dst_ref=pieces_in.at[f0],
                send_sem=piece_send.at[0], recv_sem=piece_recv.at[f0],
                device_id=group_at(f), device_id_type=MESH,
            ).wait_recv()

        cols = pl.ds(128 * f0, 128)
        for p in range(DEEP):
            for w in range(2):
                field[1, p, w, :, cols] = pieces_in[f0, w, p]
                field[0, p, w, :, cols] = pieces_in[f0, 2 + w, p]
            cour[p, :, cols] = pieces_in[f0, 4, p]

    def z_copy(s, up):
        return pltpu.make_async_remote_copy(
            src_ref=planes.at[s, DEEP - 1 if up else 0],
            dst_ref=(lo if up else hi).at[s],
            send_sem=zsend.at[s, int(up)],
            recv_sem=zrecv.at[s, int(up)],
            device_id=layer_at(layer + 1 if up else layer - 1),
            device_id_type=MESH,
        )

    def y_copy(s, down):
        return pltpu.make_async_remote_copy(
            src_ref=yout.at[s, int(down)],
            dst_ref=yin.at[s, int(down)],
            send_sem=ysend.at[s, int(down)],
            recv_sem=yrecv.at[s, int(down)],
            device_id=strip_at(strip + 1 if down else strip - 1),
            device_id_type=MESH,
        )

    directions = (
        (has_hi, z_copy, True), (has_lo, z_copy, False), (has_bottom, y_copy, True), (has_top, y_copy, False)
    )

    def publish(s, p, values):
        planes[s, p] = jnp.concatenate(values, axis=0).astype(BF16)
        for w in range(2):
            yout[s, 0, pl.ds(2 * p + w, 1), :] = values[w][0:1]
            yout[s, 1, pl.ds(2 * p + w, 1), :] = values[w][WIDE - 1 : WIDE]

    def send(s):
        for present, copy, forward in directions:
            @pl.when(present)
            def _(copy=copy, forward=forward):
                copy(s, forward).start()

    def spec_copy(o, k):
        return pltpu.make_async_remote_copy(
            src_ref=outgoing.at[o, k],
            dst_ref=fresh.at[f, k],
            send_sem=spec_send.at[o, k],
            recv_sem=spec_recv.at[f, k],
            device_id=group_at(peers[o]),
            device_id_type=MESH,
        )

    def send_spectra(k):
        for o in range(NF - 1):
            for w in range(2):
                outgoing[o, k, w] = turned(raw[o, w, k]).astype(BF16)
            spec_copy(o, k).start()
        for w in range(2):
            fresh[f, k, w] = turned(raw[NF - 1, w, k]).astype(BF16)

    def held_copy(n, batch):
        return pltpu.make_async_remote_copy(
            src_ref=planes.at[pl.ds(4 * batch + 1, 4), mates[n]],
            dst_ref=held.at[pl.ds(4 * batch, 4), wide],
            send_sem=held_send.at[batch, n],
            recv_sem=held_recv.at[batch, wide],
            device_id=plane_at(mates[n]),
            device_id_type=MESH,
        )

    for p in range(DEEP):
        publish(0, p, [field[0, p, w] for w in range(2)])
    send(0)

    source = src_ref[0]
    source_row = ((source >> 9) & (NY - 1)) - first_row
    source_plane = (source >> 16) - first_plane
    at_source = (row_id == source_row) & (col_id == (source & (COLS - 1)))

    def arrivals(s, present, copy, there):
        @pl.when(present)
        def _():
            copy.wait_recv()

        @pl.when(jnp.logical_not(present))
        def _():
            there[s] = jnp.zeros(there.shape[1:], there.dtype)

    def advance(t, carry):
        now, other = t % 2, (t + 1) % 2

        @pl.when(t < BESIDE)
        def _():
            send_spectra(t)

        arrivals(t, has_lo, z_copy(t, True), lo)
        arrivals(t, has_hi, z_copy(t, False), hi)
        arrivals(t, has_top, y_copy(t, True), yin.at[:, 1])
        arrivals(t, has_bottom, y_copy(t, False), yin.at[:, 0])
        below = [lo[t].astype(F32)[WIDE * w : WIDE * (w + 1)] for w in range(2)]
        above = [hi[t].astype(F32)[WIDE * w : WIDE * (w + 1)] for w in range(2)]
        for p in range(DEEP):
            values = []
            for w in range(2):
                u = field[now, p, w]
                beside = (field[now, p - 1, w] if p else below[w])
                beside += (field[now, p + 1, w] if p < DEEP - 1 else above[w])
                top, bottom = (yin[t, d, pl.ds(2 * p + w, 1), :] for d in (1, 0))
                beside += jnp.where(row_id == 0, top, pltpu.roll(u, 1, 0))
                beside += jnp.where(row_id == WIDE - 1, bottom, pltpu.roll(u, WIDE - 1, 0))
                beside += jnp.where(col_id == 0, 0.0, pltpu.roll(u, 1, 1))
                beside += jnp.where(col_id == COLS - 1, 0.0, pltpu.roll(u, COLS - 1, 1))
                if w == 1:
                    injection = inj[t, p]
                else:
                    injection = jnp.where(at_source & (source_plane == p), wav_ref[t], 0.0)
                following = 2.0 * u - field[other, p, w] + cour[p] * (beside - 6.0 * u) + injection
                field[other, p, w] = following
                values.append(following)
            publish(t + 1, p, values)

        @pl.when(t < STEPS - 1)
        def _():
            send(t + 1)

        held[t, wide] = planes[t + 1, wide]

        @pl.when(t % 4 == 3)
        def _():
            for n in range(3):
                held_copy(n, t // 4).start()

        return carry

    lax.fori_loop(0, STEPS, advance, 0)

    def rest(k, carry):
        send_spectra(k)
        return carry

    lax.fori_loop(BESIDE, TERMS, rest, 0)

    def turn_batch(batch, carry):
        for n in range(3):
            pltpu.make_async_remote_copy(
                src_ref=planes.at[pl.ds(4 * batch + 1, 4), mates[n]],
                dst_ref=held.at[pl.ds(4 * batch, 4), mates[n]],
                send_sem=held_send.at[batch, n], recv_sem=held_recv.at[batch, mates[n]],
                device_id=plane_at(mates[n]), device_id_type=MESH,
            ).wait_recv()

        def turn(q, inner):
            t = 4 * batch + q
            strips = held[t].astype(F32)
            for w in range(2):
                plane = turned(strips[:, WIDE * w : WIDE * (w + 1)].reshape(ROWS, COLS)).astype(BF16)
                for i in range(XS // HALF):
                    snaps[w, i // 2, t, :, pl.ds((i % 2) * XS, XS)] = plane[HALF * i : HALF * (i + 1)]
            return inner

        return lax.fori_loop(0, 4, turn, carry)

    lax.fori_loop(0, STEPS // 4, turn_batch, 0)

    offsets = [2 * lag_ref[h] + 2 * LAGMAX for h in range(lags)]
    batch = ROUND * NF

    def clear(h, carry):
        sums[h] = jnp.zeros(sums.shape[1:], F32)
        return carry

    lax.fori_loop(0, lags, clear, 0)

    def one_round(r, carry):
        def arrive(q, inner):
            k = r * ROUND + q
            for o in range(NF - 1):
                pltpu.make_async_remote_copy(
                    src_ref=outgoing.at[o, k], dst_ref=fresh.at[peers[o], k],
                    send_sem=spec_send.at[o, k], recv_sem=spec_recv.at[peers[o], k],
                    device_id=group_at(peers[o]), device_id_type=MESH,
                ).wait_recv()
            return inner

        lax.fori_loop(0, ROUND, arrive, 0)
        size = batch * HALF
        table = mix[pl.ds(pl.multiple_of(r * size, size), size), :]
        for w in range(2):
            for pair in range(XS // HALF // 2):
                moments = snaps[w, pair].reshape(STEPS * HALF, 2 * XS)
                part = jnp.dot(table, moments, preferred_element_type=F32).reshape(batch, HALF, 2 * XS)
                for q in range(ROUND):
                    for g in range(NF):
                        for i in range(2):
                            at = HALF * (2 * pair + i)
                            total = part[q * NF + g, :, XS * i : XS * (i + 1)]
                            total += fresh[g, r * ROUND + q, w, pl.ds(at, HALF), :].astype(F32)
                            if w == 0:
                                early[q * NF + g, pl.ds(at, HALF), :] = total
                            else:
                                late[q * NF + g, pl.ds(at + 2 * LAGMAX, HALF), :] = total

        def wrap(k, inner):
            late[k, pl.ds(0, 2 * LAGMAX), :] = pltpu.roll(late[k, pl.ds(XS, 2 * LAGMAX), :], ROWS, 1)
            late[k, pl.ds(XS + 2 * LAGMAX, 2 * LAGMAX), :] = pltpu.roll(
                late[k, pl.ds(2 * LAGMAX, 2 * LAGMAX), :], XS - ROWS, 1
            )
            return inner

        lax.fori_loop(0, batch, wrap, 0)

        def tile(i, inner):
            at = pl.multiple_of(i * HALF, HALF)
            starts = [at + offset for offset in offsets]

            def add(k, totals):
                for step in range(4):
                    one = early[4 * k + step, pl.ds(at, HALF), :]
                    totals = tuple(
                        total + one * late[4 * k + step, pl.ds(start, HALF), :]
                        for total, start in zip(totals, starts)
                    )
                return totals

            totals = lax.fori_loop(
                0, batch // 4, add, tuple(sums[h, pl.ds(at + LAGMAX, HALF), :] for h in range(lags))
            )
            for h in range(lags):
                sums[h, pl.ds(at + LAGMAX, HALF), :] = totals[h]
            return inner

        return lax.fori_loop(0, XS // HALF, tile, carry)

    lax.fori_loop(0, TERMS // ROUND, one_round, 0)

    x = (
        lax.broadcasted_iota(jnp.int32, (XS, XS), 0)
        + lax.broadcasted_iota(jnp.int32, (XS, XS), 1) // ROWS * XS
    )
    weight = 1.0 / (STEPS * terms / 2)

    def finish(h, carry):
        lag = lag_ref[h]
        sums[h, pl.ds(0, LAGMAX), :] = pltpu.roll(sums[h, pl.ds(XS, LAGMAX), :], ROWS, 1)
        sums[h, pl.ds(XS + LAGMAX, LAGMAX), :] = pltpu.roll(sums[h, pl.ds(LAGMAX, LAGMAX), :], XS - ROWS, 1)
        moved = sums[h, pl.ds(LAGMAX - lag, XS), :]
        reach = jnp.abs(lag)
        kept = jnp.where((x >= reach) & (x < COLS - reach), moved * weight, 0.0).T
        for c in range(BLOCKS):
            out[h, :, pl.ds(XS * c, XS)] = kept[ROWS * c : ROWS * (c + 1)].astype(BF16)
        return carry

    lax.fori_loop(0, lags, finish, 0)

    def sent(s, carry):
        for present, copy, forward in directions:
            @pl.when(present)
            def _(copy=copy, forward=forward):
                copy(s, forward).wait_send()

        for o in range(NF - 1):
            spec_copy(o, s).wait_send()
        return carry

    lax.fori_loop(0, STEPS, sent, 0)

    def delivered(batch, carry):
        for n in range(3):
            held_copy(n, batch).wait_send()
        return carry

    lax.fori_loop(0, STEPS // 4, delivered, 0)

    for group in range(4):
        @pl.when(jnp.logical_not(mine & (deep == group)))
        def _(group=group):
            piece_copy(group).wait_send()


def body(
    previous_field, current_field, courant, wavelet, traces, source_cell, receiver_cells,
    frequency_list, lag_list, spectra,
):
    lags, terms = lag_list.shape[0], NF * TERMS
    table = dft_table(frequency_list).reshape(STEPS, NF, TERMS).transpose(2, 1, 0).reshape(terms, STEPS)
    vmem = pl.BlockSpec(memory_space=pltpu.VMEM)
    smem = pl.BlockSpec(memory_space=pltpu.SMEM)
    dma = pltpu.SemaphoreType.DMA
    pair = (2 * WIDE, COLS)
    image = pl.pallas_call(
        kernel,
        out_shape=jax.ShapeDtypeStruct((lags, ROWS, COLS), BF16),
        in_specs=[vmem, vmem, vmem, smem, vmem, smem, vmem, smem, vmem, pl.BlockSpec(memory_space=pl.ANY)],
        out_specs=vmem,
        scratch_shapes=[
            pltpu.VMEM((NF, 2, TERMS, ROWS, COLS), F32),
            pltpu.VMEM((NF - 1, TERMS, 2, XS, XS), BF16),
            pltpu.VMEM((NF, TERMS, 2, XS, XS), BF16),
            pltpu.VMEM((4, 5, DEEP, WIDE, 128), F32),
            pltpu.VMEM((NF, 5, DEEP, WIDE, 128), F32),
            pltpu.VMEM((2, DEEP, 2, WIDE, COLS), F32),
            pltpu.VMEM((DEEP, WIDE, COLS), F32),
            pltpu.VMEM((STEPS, DEEP, WIDE, COLS), F32),
            pltpu.VMEM((STEPS + 1, DEEP) + pair, BF16),
            pltpu.VMEM((STEPS, 4) + pair, BF16),
            pltpu.VMEM((STEPS,) + pair, BF16),
            pltpu.VMEM((STEPS,) + pair, BF16),
            pltpu.VMEM((STEPS + 1, 2, 2 * DEEP, COLS), F32),
            pltpu.VMEM((STEPS, 2, 2 * DEEP, COLS), F32),
            pltpu.VMEM((terms, STEPS * HALF), F32),
            pltpu.VMEM((terms * HALF, STEPS * HALF), BF16),
            pltpu.VMEM((2, XS // HALF // 2, STEPS, HALF, 2 * XS), BF16),
            pltpu.VMEM((ROUND * NF, XS, XS), F32),
            pltpu.VMEM((ROUND * NF, XS + 4 * LAGMAX, XS), F32),
            pltpu.VMEM((lags, XS + 2 * LAGMAX, XS), F32),
            dma((NF, 2)),
            dma((NF - 1, TERMS)),
            dma((NF, TERMS)),
            dma((4,)),
            dma((NF,)),
            dma((STEPS, 2)),
            dma((STEPS, 2)),
            dma((STEPS, 2)),
            dma((STEPS, 2)),
            dma((STEPS // 4, 3)),
            dma((STEPS // 4, 4)),
        ],
        compiler_params=pltpu.CompilerParams(
            collective_id=0, has_side_effects=True, vmem_limit_bytes=56 * 2**20
        ),
        name="window_image",
    )(
        previous_field, current_field, courant, wavelet, traces, source_cell,
        receiver_cells.reshape(1, -1), lag_list, table, spectra.reshape(2, TERMS, NY, COLS),
    )
    return image.reshape(lags, 1, 1, ROWS, COLS)


def solution(mesh):
    placed = (
        P(None, "xy", "slab", "freq"),
        P(None, "xy", "slab", "freq"),
        P("xy", "slab", "freq"),
        P(),
        P(),
        P(),
        P(),
        P(),
        P(),
        P(None, "freq", None, "xy", "slab", None, None),
    )
    return jax.shard_map(
        body,
        mesh=mesh,
        in_specs=placed,
        out_specs=P(None, "xy", "slab", "freq", None),
        check_vma=False,
    )
```

```python
import math

import jax
import jax.numpy as jnp
from jax import lax
from jax.experimental import pallas as pl
from jax.experimental.pallas import tpu as pltpu
from jax.sharding import PartitionSpec as P

STEPS = 16
NTOT = 2048
LAGMAX = 16
NF, NS, NB = 4, 16, 4
ROWS, COLS = 32, 512
DEEP, WIDE = 4, 8
RING = 16
TERMS = 16
NY = NF * ROWS
F32, BF16 = jnp.float32, jnp.bfloat16
XS = 128
BLOCKS = COLS // XS
HALF = 16
ROUND = 2
ROUNDS = STEPS // 2
AHEAD, EACH, BESIDE = 2, 1, 10
MESH = pl.DeviceIdType.MESH


def dft_table(frequency_list):
    moments = jnp.arange(STEPS, dtype=jnp.int32) + (NTOT - STEPS)
    phase_index = moments[:, None] * frequency_list[None, :] % NTOT
    phase_angle = phase_index.astype(F32) * (2.0 * math.pi / NTOT)
    return jnp.stack([jnp.cos(phase_angle), -jnp.sin(phase_angle)], axis=-1).astype(BF16)


def swung(outer, inner):
    return inner + outer % 2 * (3 - 2 * inner)


def turned(rows):
    return jnp.concatenate([rows[:, XS * c : XS * (c + 1)] for c in range(BLOCKS)], axis=0).T


def kernel(
    prev_ref, cur_ref, cour_ref, wav_ref, traces_ref, src_ref, rec_ref, lag_ref, table_ref, spec_ref,
    out,
    raw, outgoing, fresh, pieces_out, pieces_in, field, cour, inj, planes, held, lo, hi, yout, yin, corner_out, corner, first_z, first_y, first_lo, first_hi, first_in,
    spread, mix, snaps, early, late, sums,
    raw_sem, spec_send, spec_recv, piece_send, piece_recv,
    zsend, zrecv, ysend, yrecv, csend, crecv, fsend, frecv, held_send, held_recv,
):
    f, j, b = lax.axis_index("freq"), lax.axis_index("slab"), lax.axis_index("xy")
    home, post = j // 4, j % 4
    deep, wide = swung(b, home), swung(f, post)
    layer, strip = b * 4 + deep, f * 4 + wide
    first_plane, first_row = layer * DEEP, strip * WIDE
    has_lo, has_hi = layer > 0, layer < NB * 4 - 1
    has_top, has_bottom = strip > 0, strip < NF * 4 - 1
    lags = lag_ref.shape[0]

    def block_at(up, down):
        to_layer, to_strip = layer + up, strip + down
        return {
            "freq": to_strip // 4,
            "slab": swung(to_layer // 4, to_layer % 4) * 4 + swung(to_strip // 4, to_strip % 4),
            "xy": to_layer // 4,
        }

    def group_at(other):
        return {"freq": other, "slab": j, "xy": b}

    def plane_at(other):
        return {"freq": f, "slab": deep * 4 + other, "xy": b}

    peers = (lax.rem(f + 2, NF), NF - 1 - f, f + 1 - 2 * lax.rem(f, 2))
    chunk = peers + (f,)
    owns = b % 2 == 0

    def raw_copy(o, w):
        return pltpu.make_async_copy(
            spec_ref.at[w, :, pl.ds(chunk[o] * ROWS, ROWS), :], raw.at[o, w], raw_sem.at[o, w]
        )

    for o in range(NF):
        for w in range(2):
            raw_copy(o, w).start()

    barrier = pltpu.get_barrier_semaphore()
    mine = (home == f) & (f % 2 == 0)

    def greet(there):
        pl.semaphore_signal(barrier, 1, device_id=there, device_id_type=MESH)

    for p in peers:
        greet(group_at(p))
    for n in range(4):
        @pl.when(jnp.logical_not(owns & (post == n)))
        def _(n=n):
            greet(plane_at(n))

    sides = (
        (has_hi, 1, 0), (has_lo, -1, 0), (has_bottom, 0, 1), (has_top, 0, -1),
        (has_hi & has_bottom, 1, 1), (has_hi & has_top, 1, -1),
        (has_lo & has_bottom, -1, 1), (has_lo & has_top, -1, -1),
    )
    for present, up, down in sides:
        @pl.when(present)
        def _(up=up, down=down):
            greet(block_at(up, down))

    for f0 in range(NF):
        @pl.when(jnp.logical_not(mine & (f == f0)))
        def _(f0=f0):
            greet({"freq": f0, "slab": 4 * f + wide, "xy": b})

    def stack(i, carry):
        group, p = i // DEEP, i % DEEP
        for w in range(2):
            pieces_out[group, w, p] = prev_ref[w, i]
            pieces_out[group, 2 + w, p] = cur_ref[w, i]
        pieces_out[group, 4, p] = cour_ref[i]
        return carry

    lax.fori_loop(0, NS, stack, 0)

    expected = len(peers) + 4 + NF - mine.astype(jnp.int32) - owns.astype(jnp.int32)
    for present, _, _ in sides:
        expected += present.astype(jnp.int32)
    pl.semaphore_wait(barrier, expected)

    def piece_copy(group):
        return pltpu.make_async_remote_copy(
            src_ref=pieces_out.at[group],
            dst_ref=pieces_in.at[f],
            send_sem=piece_send.at[group],
            recv_sem=piece_recv.at[f],
            device_id={"freq": home, "slab": 4 * swung(b, group) + swung(home, post), "xy": b},
            device_id_type=MESH,
        )

    for group in range(4):
        @pl.when(jnp.logical_not(mine & (deep == group)))
        def _(group=group):
            piece_copy(group).start()

    @pl.when(mine)
    def _():
        pieces_in[f] = pieces_out[deep]

    def spec_copy(o, k):
        return pltpu.make_async_remote_copy(
            src_ref=outgoing.at[o, k],
            dst_ref=fresh.at[f, k],
            send_sem=spec_send.at[o, k],
            recv_sem=spec_recv.at[f, k],
            device_id=group_at(peers[o]),
            device_id_type=MESH,
        )

    def send_spectra(k):
        for o in range(NF - 1):
            for w in range(2):
                outgoing[o, k, w] = turned(raw[o, w, k]).astype(BF16)
            spec_copy(o, k).start()
        for w in range(2):
            fresh[f, k, w] = turned(raw[NF - 1, w, k]).astype(BF16)

    for o in range(NF):
        for w in range(2):
            raw_copy(o, w).wait()

    for k in range(AHEAD):
        send_spectra(k)

    cell = rec_ref[...]
    depth, row, col = (cell >> 16) - first_plane + 1, ((cell >> 9) & (NY - 1)) - first_row, cell & (COLS - 1)
    here = (depth >= 0) & (depth < DEEP + 2) & (row >= -1) & (row <= WIDE)
    row = jnp.where(here, depth * RING + (row & (RING - 1)), -1)
    size = (DEEP + 2) * RING
    at_row = lax.broadcasted_iota(jnp.int32, (size, cell.shape[1]), 0) == row
    at_col = (lax.broadcasted_iota(jnp.int32, (COLS, cell.shape[1]), 0) == col).astype(F32).astype(BF16)

    def inject(t, carry):
        values = jnp.where(at_row, traces_ref[pl.ds(t, 1), :], 0.0)
        first = values.astype(BF16)
        rest = values - first.astype(F32)
        second = rest.astype(BF16)
        third = (rest - second.astype(F32)).astype(BF16)
        parts = lax.dot_general(
            jnp.concatenate([first, second, third], axis=0), at_col,
            (((1,), (1,)), ((), ())), preferred_element_type=F32,
        )
        total = parts[:size] + parts[size : 2 * size] + parts[2 * size :]
        inj[t] = total.reshape(DEEP + 2, RING, COLS)
        return carry

    terms = NF * TERMS
    step_of = lax.broadcasted_iota(jnp.int32, (STEPS, STEPS * HALF), 1) // HALF
    chosen = (step_of == lax.broadcasted_iota(jnp.int32, (STEPS, STEPS * HALF), 0)).astype(F32).astype(BF16)
    spread[...] = jnp.dot(table_ref[...], chosen, preferred_element_type=F32)
    place = lax.broadcasted_iota(jnp.int32, (HALF, STEPS * HALF), 1) % HALF
    diagonal = place == lax.broadcasted_iota(jnp.int32, (HALF, STEPS * HALF), 0)

    def fill(k, carry):
        values = jnp.where(diagonal, spread[pl.ds(k, 1), :], 0.0)
        mix[pl.ds(pl.multiple_of(k * HALF, HALF), HALF), :] = values.astype(BF16)
        return carry

    def clear_plane(p, carry):
        for n in range(2):
            for w in range(2):
                field[n, p, w] = jnp.zeros((RING, COLS), F32)

        @pl.when(p < DEEP + 2)
        def _():
            cour[p] = jnp.zeros((RING, COLS), F32)

        return carry

    lax.fori_loop(0, DEEP + 4, clear_plane, 0)

    for f0 in range(NF):
        @pl.when(jnp.logical_not(mine & (f == f0)))
        def _(f0=f0):
            pltpu.make_async_remote_copy(
                src_ref=pieces_out.at[0], dst_ref=pieces_in.at[f0],
                send_sem=piece_send.at[0], recv_sem=piece_recv.at[f0],
                device_id=group_at(f), device_id_type=MESH,
            ).wait_recv()

        cols = pl.ds(128 * f0, 128)
        for p in range(DEEP):
            for w in range(2):
                field[1, p + 2, w, pl.ds(0, WIDE), cols] = pieces_in[f0, w, p]
                field[0, p + 2, w, pl.ds(0, WIDE), cols] = pieces_in[f0, 2 + w, p]
            cour[p + 1, pl.ds(0, WIDE), cols] = pieces_in[f0, 4, p]

    def halo_copy(r, up, down):
        if not down:
            low = up > 0
            src, dst = planes.at[2 * r, pl.ds(DEEP - 2 if low else 0, 2)], (lo if low else hi).at[r]
            sems = zsend.at[r, int(low)], zrecv.at[r, int(low)]
        elif not up:
            n = int(down > 0)
            src, dst, sems = yout.at[r, n], yin.at[r, n], (ysend.at[r, n], yrecv.at[r, n])
        else:
            n, m = int(down > 0), int(up > 0)
            src, dst = corner_out.at[r, m, n], corner.at[r, m, n]
            sems = csend.at[r, 2 * m + n], crecv.at[r, 2 * m + n]
        return pltpu.make_async_remote_copy(
            src_ref=src, dst_ref=dst, send_sem=sems[0], recv_sem=sems[1],
            device_id=block_at(up, down), device_id_type=MESH,
        )

    def first_copy(up, down):
        n = int(up + down > 0)
        if up:
            src, dst, m = first_z.at[n], (first_lo if n else first_hi), n
        else:
            src, dst, m = first_y.at[n], first_in.at[n], 2 + n
        return pltpu.make_async_remote_copy(
            src_ref=src, dst_ref=dst, send_sem=fsend.at[m], recv_sem=frecv.at[m],
            device_id=block_at(up, down), device_id_type=MESH,
        )

    def publish(s, p, values):
        planes[s, p] = jnp.concatenate(values, axis=0).astype(BF16)

    def send(r, values):
        for present, up, down in sides[:2]:
            @pl.when(present)
            def _(up=up, down=down):
                halo_copy(r, up, down).start()

        for n, at in ((0, 0), (1, WIDE - 2)):
            rows = [values[p][w][at : at + 2] for p in range(DEEP) for w in range(2)]
            yout[r, n] = jnp.concatenate(rows, axis=0).astype(BF16)
        for m, p in ((0, 0), (1, DEEP - 1)):
            for n, at in ((0, 0), (1, WIDE - 1)):
                rows = [
                    values[p][w][at : at + 1, 128 * c : 128 * (c + 1)] for w in range(2) for c in range(4)
                ]
                corner_out[r, m, n] = jnp.concatenate(rows, axis=0)
        for present, up, down in sides[2:]:
            @pl.when(present)
            def _(up=up, down=down):
                halo_copy(r, up, down).start()

    def held_copy(n, batch):
        return pltpu.make_async_remote_copy(
            src_ref=planes.at[pl.ds(4 * batch + 1, 4), n],
            dst_ref=held.at[pl.ds(4 * batch, 4), wide],
            send_sem=held_send.at[batch, n],
            recv_sem=held_recv.at[batch, wide],
            device_id=plane_at(n),
            device_id_type=MESH,
        )

    initial = [[field[0, p + 2, w, pl.ds(0, WIDE), :] for w in range(2)] for p in range(DEEP)]
    for p in range(DEEP):
        publish(0, p, initial[p])
    send(0, initial)

    for n, p, row in ((0, 0, 0), (1, DEEP - 1, WIDE - 1)):
        for w in range(2):
            first_z[n, w] = field[1, p + 2, w, pl.ds(0, WIDE), :]
            for q in range(DEEP):
                first_y[n, pl.ds(DEEP * w + q, 1), :] = field[1, q + 2, w, pl.ds(row, 1), :]
        first_z[n, 2] = cour[p + 1, pl.ds(0, WIDE), :]
        for q in range(DEEP):
            first_y[n, pl.ds(2 * DEEP + q, 1), :] = cour[q + 1, pl.ds(row, 1), :]
        first_y[n, pl.ds(3 * DEEP, DEEP), :] = jnp.zeros((DEEP, COLS), F32)
    for present, up, down in sides[:4]:
        @pl.when(present)
        def _(up=up, down=down):
            first_copy(up, down).start()

    for present, up, down in sides[:4]:
        @pl.when(present)
        def _(up=up, down=down):
            first_copy(-up, -down).wait_recv()
            if up:
                there, at = (first_hi, DEEP + 2) if up > 0 else (first_lo, 1)
                for w in range(2):
                    field[1, at, w, pl.ds(0, WIDE), :] = there[w]
                cour[at - 1, pl.ds(0, WIDE), :] = there[2]
            else:
                n, at = (0, WIDE) if down > 0 else (1, RING - 1)
                for q in range(DEEP):
                    for w in range(2):
                        field[1, q + 2, w, pl.ds(at, 1), :] = first_in[n, pl.ds(DEEP * w + q, 1), :]
                    cour[q + 1, pl.ds(at, 1), :] = first_in[n, pl.ds(2 * DEEP + q, 1), :]

    row_id = lax.broadcasted_iota(jnp.int32, (RING, COLS), 0)
    col_id = lax.broadcasted_iota(jnp.int32, (RING, COLS), 1)
    source = src_ref[0]
    source_row = ((source >> 9) & (NY - 1)) - first_row
    source_row = jnp.where((source_row >= -1) & (source_row <= WIDE), source_row & (RING - 1), -1)
    source_plane = (source >> 16) - first_plane + 2
    at_source = (row_id == source_row) & (col_id == (source & (COLS - 1)))

    def step(t, now, p, w, height):
        u = field[now, p, w]
        beside = pltpu.roll(u, 1, 0)[:height] + pltpu.roll(u, RING - 1, 0)[:height]
        u = u[:height]
        beside += field[now, p - 1, w, pl.ds(0, height), :] + field[now, p + 1, w, pl.ds(0, height), :]
        col = col_id[:height]
        beside += jnp.where(col == 0, 0.0, pltpu.roll(u, 1, 1))
        beside += jnp.where(col == COLS - 1, 0.0, pltpu.roll(u, COLS - 1, 1))
        if w == 1:
            injection = inj[t, p - 1, pl.ds(0, height), :]
        else:
            injection = jnp.where(at_source[:height] & (source_plane == p), wav_ref[t], 0.0)
        before = field[1 - now, p, w, pl.ds(0, height), :]
        following = 2.0 * u - before + cour[p - 1, pl.ds(0, height), :] * (beside - 6.0 * u) + injection
        field[1 - now, p, w, pl.ds(0, height), :] = following
        return following

    def advance(r, carry):
        for i in range(EACH):
            k = AHEAD + EACH * r + i

            @pl.when(k < BESIDE)
            def _(k=k):
                send_spectra(k)

        lax.fori_loop(2 * r, 2 * r + 2, inject, 0)
        share = terms // ROUNDS
        lax.fori_loop(share * r, share * (r + 1), fill, 0)

        for present, up, down in sides:
            @pl.when(present)
            def _(up=up, down=down):
                halo_copy(r, -up, -down).wait_recv()
                if not down:
                    there, at = (hi, DEEP + 2) if up > 0 else (lo, 0)
                    for q in range(2):
                        both = there[r, q].astype(F32)
                        for w in range(2):
                            field[0, at + q, w, pl.ds(0, WIDE), :] = both[WIDE * w : WIDE * (w + 1)]
                    return
                n, at = (0, WIDE) if down > 0 else (1, RING - 2)
                if not up:
                    rows = yin[r, n].astype(F32)
                    for p in range(DEEP):
                        for w in range(2):
                            i = 4 * p + 2 * w
                            field[0, p + 2, w, pl.ds(at, 2), :] = rows[i : i + 2]
                else:
                    m, q = (0, DEEP + 2) if up > 0 else (1, 1)
                    at = WIDE if down > 0 else RING - 1
                    for w in range(2):
                        for c in range(4):
                            field[0, q, w, pl.ds(at, 1), pl.ds(128 * c, 128)] = corner[
                                r, m, n, pl.ds(4 * w + c, 1), :
                            ]

        t = 2 * r
        middle = [
            [step(t, 0, p, w, RING if 1 < p < DEEP + 2 else WIDE) for w in range(2)]
            for p in range(1, DEEP + 3)
        ]
        last = [[step(t + 1, 1, p, w, WIDE) for w in range(2)] for p in range(2, DEEP + 2)]
        for p in range(DEEP):
            publish(t + 2, p, last[p])

        @pl.when(r < ROUNDS - 1)
        def _():
            send(r + 1, last)

        for p in range(DEEP):
            publish(t + 1, p, [values[:WIDE] for values in middle[p + 1]])

        @pl.when(owns)
        def _():
            for i in (1, 2):
                held[t + i - 1, wide] = planes[t + i, post]

        for n in range(4):
            @pl.when((r % 2 == 1) & jnp.logical_not(owns & (post == n)))
            def _(n=n):
                held_copy(n, r // 2).start()

        return carry

    lax.fori_loop(0, ROUNDS, advance, 0)

    def rest(k, carry):
        send_spectra(k)
        return carry

    lax.fori_loop(BESIDE, TERMS, rest, 0)

    def turn_batch(batch, carry):
        for n in range(4):
            @pl.when(jnp.logical_not(owns & (post == n)))
            def _(n=n):
                pltpu.make_async_remote_copy(
                    src_ref=planes.at[pl.ds(4 * batch + 1, 4), n],
                    dst_ref=held.at[pl.ds(4 * batch, 4), swung(f, n)],
                    send_sem=held_send.at[batch, n], recv_sem=held_recv.at[batch, swung(f, n)],
                    device_id=plane_at(n), device_id_type=MESH,
                ).wait_recv()

        def turn(q, inner):
            t = 4 * batch + q
            strips = held[t].astype(F32)
            for w in range(2):
                plane = turned(strips[:, WIDE * w : WIDE * (w + 1)].reshape(ROWS, COLS)).astype(BF16)
                for i in range(XS // HALF):
                    snaps[w, i // 2, t, :, pl.ds((i % 2) * XS, XS)] = plane[HALF * i : HALF * (i + 1)]
            return inner

        return lax.fori_loop(0, 4, turn, carry)

    lax.fori_loop(0, STEPS // 4, turn_batch, 0)

    offsets = [2 * lag_ref[h] + 2 * LAGMAX for h in range(lags)]
    batch = ROUND * NF

    def clear(h, carry):
        sums[h] = jnp.zeros(sums.shape[1:], F32)
        return carry

    lax.fori_loop(0, lags, clear, 0)

    def one_round(r, carry):
        def arrive(q, inner):
            k = r * ROUND + q
            for o in range(NF - 1):
                pltpu.make_async_remote_copy(
                    src_ref=outgoing.at[o, k], dst_ref=fresh.at[peers[o], k],
                    send_sem=spec_send.at[o, k], recv_sem=spec_recv.at[peers[o], k],
                    device_id=group_at(peers[o]), device_id_type=MESH,
                ).wait_recv()
            return inner

        lax.fori_loop(0, ROUND, arrive, 0)
        size = batch * HALF
        table = mix[pl.ds(pl.multiple_of(r * size, size), size), :]
        for w in range(2):
            for pair in range(XS // HALF // 2):
                moments = snaps[w, pair].reshape(STEPS * HALF, 2 * XS)
                part = jnp.dot(table, moments, preferred_element_type=F32).reshape(batch, HALF, 2 * XS)
                for q in range(ROUND):
                    for g in range(NF):
                        for i in range(2):
                            at = HALF * (2 * pair + i)
                            total = part[q * NF + g, :, XS * i : XS * (i + 1)]
                            total += fresh[g, r * ROUND + q, w, pl.ds(at, HALF), :].astype(F32)
                            if w == 0:
                                early[q * NF + g, pl.ds(at, HALF), :] = total
                            else:
                                late[q * NF + g, pl.ds(at + 2 * LAGMAX, HALF), :] = total

        def wrap(k, inner):
            late[k, pl.ds(0, 2 * LAGMAX), :] = pltpu.roll(late[k, pl.ds(XS, 2 * LAGMAX), :], ROWS, 1)
            late[k, pl.ds(XS + 2 * LAGMAX, 2 * LAGMAX), :] = pltpu.roll(
                late[k, pl.ds(2 * LAGMAX, 2 * LAGMAX), :], XS - ROWS, 1
            )
            return inner

        lax.fori_loop(0, batch, wrap, 0)

        def tile(i, inner):
            at = pl.multiple_of(i * HALF, HALF)
            starts = [at + offset for offset in offsets]

            def add(k, totals):
                for step in range(4):
                    one = early[4 * k + step, pl.ds(at, HALF), :]
                    totals = tuple(
                        total + one * late[4 * k + step, pl.ds(start, HALF), :]
                        for total, start in zip(totals, starts)
                    )
                return totals

            totals = lax.fori_loop(
                0, batch // 4, add, tuple(sums[h, pl.ds(at + LAGMAX, HALF), :] for h in range(lags))
            )
            for h in range(lags):
                sums[h, pl.ds(at + LAGMAX, HALF), :] = totals[h]
            return inner

        return lax.fori_loop(0, XS // HALF, tile, carry)

    lax.fori_loop(0, TERMS // ROUND, one_round, 0)

    x = (
        lax.broadcasted_iota(jnp.int32, (XS, XS), 0)
        + lax.broadcasted_iota(jnp.int32, (XS, XS), 1) // ROWS * XS
    )
    weight = 1.0 / (STEPS * terms / 2)

    def finish(h, carry):
        lag = lag_ref[h]
        sums[h, pl.ds(0, LAGMAX), :] = pltpu.roll(sums[h, pl.ds(XS, LAGMAX), :], ROWS, 1)
        sums[h, pl.ds(XS + LAGMAX, LAGMAX), :] = pltpu.roll(sums[h, pl.ds(LAGMAX, LAGMAX), :], XS - ROWS, 1)
        moved = sums[h, pl.ds(LAGMAX - lag, XS), :]
        reach = jnp.abs(lag)
        kept = jnp.where((x >= reach) & (x < COLS - reach), moved * weight, 0.0).T
        for c in range(BLOCKS):
            out[h, :, pl.ds(XS * c, XS)] = kept[ROWS * c : ROWS * (c + 1)].astype(BF16)
        return carry

    lax.fori_loop(0, lags, finish, 0)

    def sent(r, carry):
        for present, up, down in sides:
            @pl.when(present)
            def _(up=up, down=down):
                halo_copy(r, up, down).wait_send()

        return carry

    lax.fori_loop(0, ROUNDS, sent, 0)

    for present, up, down in sides[:4]:
        @pl.when(present)
        def _(up=up, down=down):
            first_copy(up, down).wait_send()

    def spectra_sent(k, carry):
        for o in range(NF - 1):
            spec_copy(o, k).wait_send()
        return carry

    lax.fori_loop(0, TERMS, spectra_sent, 0)

    def delivered(batch, carry):
        for n in range(4):
            @pl.when(jnp.logical_not(owns & (post == n)))
            def _(n=n):
                held_copy(n, batch).wait_send()

        return carry

    lax.fori_loop(0, STEPS // 4, delivered, 0)

    for group in range(4):
        @pl.when(jnp.logical_not(mine & (deep == group)))
        def _(group=group):
            piece_copy(group).wait_send()


def body(
    previous_field, current_field, courant, wavelet, traces, source_cell, receiver_cells,
    frequency_list, lag_list, spectra,
):
    lags, terms = lag_list.shape[0], NF * TERMS
    table = dft_table(frequency_list).reshape(STEPS, NF, TERMS).transpose(2, 1, 0).reshape(terms, STEPS)
    vmem = pl.BlockSpec(memory_space=pltpu.VMEM)
    smem = pl.BlockSpec(memory_space=pltpu.SMEM)
    dma = pltpu.SemaphoreType.DMA
    pair = (2 * WIDE, COLS)
    image = pl.pallas_call(
        kernel,
        out_shape=jax.ShapeDtypeStruct((lags, ROWS, COLS), BF16),
        in_specs=[vmem, vmem, vmem, smem, vmem, smem, vmem, smem, vmem, pl.BlockSpec(memory_space=pl.ANY)],
        out_specs=vmem,
        scratch_shapes=[
            pltpu.VMEM((NF, 2, TERMS, ROWS, COLS), F32),
            pltpu.VMEM((NF - 1, TERMS, 2, XS, XS), BF16),
            pltpu.VMEM((NF, TERMS, 2, XS, XS), BF16),
            pltpu.VMEM((4, 5, DEEP, WIDE, 128), F32),
            pltpu.VMEM((NF, 5, DEEP, WIDE, 128), F32),
            pltpu.VMEM((2, DEEP + 4, 2, RING, COLS), F32),
            pltpu.VMEM((DEEP + 2, RING, COLS), F32),
            pltpu.VMEM((STEPS, DEEP + 2, RING, COLS), F32),
            pltpu.VMEM((STEPS + 1, DEEP) + pair, BF16),
            pltpu.VMEM((STEPS, 4) + pair, BF16),
            pltpu.VMEM((ROUNDS, 2) + pair, BF16),
            pltpu.VMEM((ROUNDS, 2) + pair, BF16),
            pltpu.VMEM((ROUNDS, 2, 4 * DEEP, COLS), BF16),
            pltpu.VMEM((ROUNDS, 2, 4 * DEEP, COLS), BF16),
            pltpu.VMEM((ROUNDS, 2, 2, 8, 128), F32),
            pltpu.VMEM((ROUNDS, 2, 2, 8, 128), F32),
            pltpu.VMEM((2, 3, WIDE, COLS), F32),
            pltpu.VMEM((2, 4 * DEEP, COLS), F32),
            pltpu.VMEM((3, WIDE, COLS), F32),
            pltpu.VMEM((3, WIDE, COLS), F32),
            pltpu.VMEM((2, 4 * DEEP, COLS), F32),
            pltpu.VMEM((terms, STEPS * HALF), F32),
            pltpu.VMEM((terms * HALF, STEPS * HALF), BF16),
            pltpu.VMEM((2, XS // HALF // 2, STEPS, HALF, 2 * XS), BF16),
            pltpu.VMEM((ROUND * NF, XS, XS), F32),
            pltpu.VMEM((ROUND * NF, XS + 4 * LAGMAX, XS), F32),
            pltpu.VMEM((lags, XS + 2 * LAGMAX, XS), F32),
            dma((NF, 2)),
            dma((NF - 1, TERMS)),
            dma((NF, TERMS)),
            dma((4,)),
            dma((NF,)),
            dma((ROUNDS, 2)),
            dma((ROUNDS, 2)),
            dma((ROUNDS, 2)),
            dma((ROUNDS, 2)),
            dma((ROUNDS, 4)),
            dma((ROUNDS, 4)),
            dma((4,)),
            dma((4,)),
            dma((STEPS // 4, 4)),
            dma((STEPS // 4, 4)),
        ],
        compiler_params=pltpu.CompilerParams(
            collective_id=0, has_side_effects=True, vmem_limit_bytes=56 * 2**20
        ),
        name="window_image",
    )(
        previous_field, current_field, courant, wavelet, traces, source_cell,
        receiver_cells.reshape(1, -1), lag_list, table, spectra.reshape(2, TERMS, NY, COLS),
    )
    return image.reshape(lags, 1, 1, ROWS, COLS)


def solution(mesh):
    placed = (
        P(None, "xy", "slab", "freq"),
        P(None, "xy", "slab", "freq"),
        P("xy", "slab", "freq"),
        P(),
        P(),
        P(),
        P(),
        P(),
        P(),
        P(None, "freq", None, "xy", "slab", None, None),
    )
    return jax.shard_map(
        body,
        mesh=mesh,
        in_specs=placed,
        out_specs=P(None, "xy", "slab", "freq", None),
        check_vma=False,
    )
```

```python
import math

import jax
import jax.numpy as jnp
from jax import lax
from jax.experimental import pallas as pl
from jax.experimental.pallas import tpu as pltpu
from jax.sharding import PartitionSpec as P

STEPS = 16
NTOT = 2048
LAGMAX = 16
NF, NS, NB = 4, 16, 4
ROWS, COLS = 32, 512
DEEP, WIDE = 4, 8
RING = 16
TERMS = 16
NY = NF * ROWS
F32, BF16 = jnp.float32, jnp.bfloat16
XS = 128
BLOCKS = COLS // XS
HALF = 16
ROUND = 2
ROUNDS = STEPS // 2
AHEAD, EACH, BESIDE = 1, 1, 9
MESH = pl.DeviceIdType.MESH


def dft_table(frequency_list):
    moments = jnp.arange(STEPS, dtype=jnp.int32) + (NTOT - STEPS)
    phase_index = moments[:, None] * frequency_list[None, :] % NTOT
    phase_angle = phase_index.astype(F32) * (2.0 * math.pi / NTOT)
    return jnp.stack([jnp.cos(phase_angle), -jnp.sin(phase_angle)], axis=-1).astype(BF16)


def swung(outer, inner):
    return inner + outer % 2 * (3 - 2 * inner)


def turned(rows):
    return jnp.concatenate([rows[:, XS * c : XS * (c + 1)] for c in range(BLOCKS)], axis=0).T


def kernel(
    prev_ref, cur_ref, cour_ref, wav_ref, traces_ref, src_ref, rec_ref, lag_ref, table_ref, spec_ref,
    out,
    raw, outgoing, fresh, pieces_out, relay, pieces_in, field, cour, inj, planes, held, lo, hi, yout, yin, corner_out, corner, first_z, first_y, first_lo, first_hi, first_in,
    spread, mix, snaps, early, late, sums,
    raw_sem, spec_send, spec_recv, relay_send, relay_recv, piece_send, piece_recv,
    zsend, zrecv, ysend, yrecv, csend, crecv, fsend, frecv, held_send, held_recv,
):
    f, j, b = lax.axis_index("freq"), lax.axis_index("slab"), lax.axis_index("xy")
    home, post = j // 4, j % 4
    deep, wide = swung(b, home), swung(f, post)
    layer, strip = b * 4 + deep, f * 4 + wide
    first_plane, first_row = layer * DEEP, strip * WIDE
    has_lo, has_hi = layer > 0, layer < NB * 4 - 1
    has_top, has_bottom = strip > 0, strip < NF * 4 - 1
    lags = lag_ref.shape[0]

    def block_at(up, down):
        to_layer, to_strip = layer + up, strip + down
        return {
            "freq": to_strip // 4,
            "slab": swung(to_layer // 4, to_layer % 4) * 4 + swung(to_strip // 4, to_strip % 4),
            "xy": to_layer // 4,
        }

    def group_at(other):
        return {"freq": other, "slab": j, "xy": b}

    def plane_at(other):
        return {"freq": f, "slab": deep * 4 + other, "xy": b}

    peers = (lax.rem(f + 2, NF), NF - 1 - f, f + 1 - 2 * lax.rem(f, 2))
    chunk = peers + (f,)
    owns = b % 2 == 0

    def raw_copy(o, w):
        return pltpu.make_async_copy(
            spec_ref.at[w, :, pl.ds(chunk[o] * ROWS, ROWS), :], raw.at[o, w], raw_sem.at[o, w]
        )

    for o in range(NF):
        for w in range(2):
            raw_copy(o, w).start()

    barrier = pltpu.get_barrier_semaphore()
    mine = f % 2 == 0

    def greet(there):
        pl.semaphore_signal(barrier, 1, device_id=there, device_id_type=MESH)

    for p in peers:
        greet(group_at(p))
    for n in range(4):
        @pl.when(jnp.logical_not(owns & (post == n)))
        def _(n=n):
            greet(plane_at(n))

    sides = (
        (has_hi, 1, 0), (has_lo, -1, 0), (has_bottom, 0, 1), (has_top, 0, -1),
        (has_hi & has_bottom, 1, 1), (has_hi & has_top, 1, -1),
        (has_lo & has_bottom, -1, 1), (has_lo & has_top, -1, -1),
    )
    for present, up, down in sides:
        @pl.when(present)
        def _(up=up, down=down):
            greet(block_at(up, down))

    for n in range(4):
        @pl.when(home != n)
        def _(n=n):
            greet({"freq": f, "slab": 4 * n + post, "xy": b})

    for f0 in range(NF):
        @pl.when(jnp.logical_not(mine & (f == f0)))
        def _(f0=f0):
            greet({"freq": f0, "slab": 4 * home + wide, "xy": b})

    def stack(group, carry):
        at = pl.ds(group * DEEP, DEEP)
        for w in range(2):
            pieces_out[group, w] = prev_ref[w, at].reshape(DEEP * WIDE, 128).astype(BF16)
            pieces_out[group, 2 + w] = cur_ref[w, at].reshape(DEEP * WIDE, 128).astype(BF16)
        pieces_out[group, 4] = cour_ref[at].reshape(DEEP * WIDE, 128).astype(BF16)
        return carry

    lax.fori_loop(0, 4, stack, 0)

    expected = len(peers) + 4 + 3 + NF - mine.astype(jnp.int32) - owns.astype(jnp.int32)
    for present, _, _ in sides:
        expected += present.astype(jnp.int32)
    pl.semaphore_wait(barrier, expected)

    def relay_copy(n):
        group = swung(b, n)
        return pltpu.make_async_remote_copy(
            src_ref=pieces_out.at[group],
            dst_ref=relay.at[home],
            send_sem=relay_send.at[n],
            recv_sem=relay_recv.at[home],
            device_id={"freq": f, "slab": 4 * n + post, "xy": b},
            device_id_type=MESH,
        )

    def piece_copy(n):
        return pltpu.make_async_remote_copy(
            src_ref=relay.at[n],
            dst_ref=pieces_in.at[f],
            send_sem=piece_send.at[n],
            recv_sem=piece_recv.at[f],
            device_id={"freq": n, "slab": 4 * home + swung(n, post), "xy": b},
            device_id_type=MESH,
        )

    for n in range(4):
        @pl.when(home != n)
        def _(n=n):
            relay_copy(n).start()

    relay[home] = pieces_out[deep]

    for n in range(4):
        @pl.when(home != n)
        def _(n=n):
            pltpu.make_async_remote_copy(
                src_ref=pieces_out.at[n], dst_ref=relay.at[n],
                send_sem=relay_send.at[n], recv_sem=relay_recv.at[n],
                device_id={"freq": f, "slab": 4 * n + post, "xy": b}, device_id_type=MESH,
            ).wait_recv()

        @pl.when(jnp.logical_not(mine & (f == n)))
        def _(n=n):
            piece_copy(n).start()

    @pl.when(mine)
    def _():
        pieces_in[f] = relay[f]

    def spec_copy(o, k):
        return pltpu.make_async_remote_copy(
            src_ref=outgoing.at[o, k],
            dst_ref=fresh.at[f, k],
            send_sem=spec_send.at[o, k],
            recv_sem=spec_recv.at[f, k],
            device_id=group_at(peers[o]),
            device_id_type=MESH,
        )

    def send_spectra(k):
        for o in range(NF - 1):
            for w in range(2):
                outgoing[o, k, w] = turned(raw[o, w, k]).astype(BF16)
            spec_copy(o, k).start()
        for w in range(2):
            fresh[f, k, w] = turned(raw[NF - 1, w, k]).astype(BF16)

    for o in range(NF):
        for w in range(2):
            raw_copy(o, w).wait()

    for k in range(AHEAD):
        send_spectra(k)

    cell = rec_ref[...]
    depth, row, col = (cell >> 16) - first_plane + 1, ((cell >> 9) & (NY - 1)) - first_row, cell & (COLS - 1)
    here = (depth >= 0) & (depth < DEEP + 2) & (row >= -1) & (row <= WIDE)
    row = jnp.where(here, depth * RING + (row & (RING - 1)), -1)
    size = (DEEP + 2) * RING
    at_row = lax.broadcasted_iota(jnp.int32, (size, cell.shape[1]), 0) == row
    at_col = (lax.broadcasted_iota(jnp.int32, (COLS, cell.shape[1]), 0) == col).astype(F32).astype(BF16)

    def inject(t, carry):
        values = jnp.where(at_row, traces_ref[pl.ds(t, 1), :], 0.0)
        first = values.astype(BF16)
        rest = values - first.astype(F32)
        second = rest.astype(BF16)
        third = (rest - second.astype(F32)).astype(BF16)
        parts = lax.dot_general(
            jnp.concatenate([first, second, third], axis=0), at_col,
            (((1,), (1,)), ((), ())), preferred_element_type=F32,
        )
        total = parts[:size] + parts[size : 2 * size] + parts[2 * size :]
        inj[t] = total.reshape(DEEP + 2, RING, COLS)
        return carry

    terms = NF * TERMS
    step_of = lax.broadcasted_iota(jnp.int32, (STEPS, STEPS * HALF), 1) // HALF
    chosen = (step_of == lax.broadcasted_iota(jnp.int32, (STEPS, STEPS * HALF), 0)).astype(F32).astype(BF16)
    spread[...] = jnp.dot(table_ref[...], chosen, preferred_element_type=F32)
    place = lax.broadcasted_iota(jnp.int32, (HALF, STEPS * HALF), 1) % HALF
    diagonal = place == lax.broadcasted_iota(jnp.int32, (HALF, STEPS * HALF), 0)

    def fill(k, carry):
        values = jnp.where(diagonal, spread[pl.ds(k, 1), :], 0.0)
        mix[pl.ds(pl.multiple_of(k * HALF, HALF), HALF), :] = values.astype(BF16)
        return carry

    def clear_plane(p, carry):
        for n in range(2):
            for w in range(2):
                field[n, p, w] = jnp.zeros((RING, COLS), F32)

        @pl.when(p < DEEP + 2)
        def _():
            cour[p] = jnp.zeros((RING, COLS), F32)

        return carry

    lax.fori_loop(0, DEEP + 4, clear_plane, 0)

    for f0 in range(NF):
        @pl.when(jnp.logical_not(mine & (f == f0)))
        def _(f0=f0):
            pltpu.make_async_remote_copy(
                src_ref=pieces_out.at[0], dst_ref=pieces_in.at[f0],
                send_sem=piece_send.at[0], recv_sem=piece_recv.at[f0],
                device_id=group_at(f), device_id_type=MESH,
            ).wait_recv()

        cols = pl.ds(128 * f0, 128)
        piece = [pieces_in[f0, n].astype(F32) for n in range(5)]
        for p in range(DEEP):
            rows = slice(WIDE * p, WIDE * (p + 1))
            for w in range(2):
                field[1, p + 2, w, pl.ds(0, WIDE), cols] = piece[w][rows]
                field[0, p + 2, w, pl.ds(0, WIDE), cols] = piece[2 + w][rows]
            cour[p + 1, pl.ds(0, WIDE), cols] = piece[4][rows]

    def halo_copy(r, up, down):
        if not down:
            low = up > 0
            src, dst = planes.at[2 * r, pl.ds(DEEP - 2 if low else 0, 2)], (lo if low else hi).at[r]
            sems = zsend.at[r, int(low)], zrecv.at[r, int(low)]
        elif not up:
            n = int(down > 0)
            src, dst, sems = yout.at[r, n], yin.at[r, n], (ysend.at[r, n], yrecv.at[r, n])
        else:
            n, m = int(down > 0), int(up > 0)
            src, dst = corner_out.at[r, m, n], corner.at[r, m, n]
            sems = csend.at[r, 2 * m + n], crecv.at[r, 2 * m + n]
        return pltpu.make_async_remote_copy(
            src_ref=src, dst_ref=dst, send_sem=sems[0], recv_sem=sems[1],
            device_id=block_at(up, down), device_id_type=MESH,
        )

    def first_copy(up, down):
        n = int(up + down > 0)
        if up:
            src, dst, m = first_z.at[n], (first_lo if n else first_hi), n
        else:
            src, dst, m = first_y.at[n], first_in.at[n], 2 + n
        return pltpu.make_async_remote_copy(
            src_ref=src, dst_ref=dst, send_sem=fsend.at[m], recv_sem=frecv.at[m],
            device_id=block_at(up, down), device_id_type=MESH,
        )

    def publish(s, p, values):
        planes[s, p] = jnp.concatenate(values, axis=0).astype(BF16)

    def send(r, values):
        for present, up, down in sides[:2]:
            @pl.when(present)
            def _(up=up, down=down):
                halo_copy(r, up, down).start()

        for n, at in ((0, 0), (1, WIDE - 2)):
            rows = [values[p][w][at : at + 2] for p in range(DEEP) for w in range(2)]
            yout[r, n] = jnp.concatenate(rows, axis=0).astype(BF16)
        for m, p in ((0, 0), (1, DEEP - 1)):
            for n, at in ((0, 0), (1, WIDE - 1)):
                rows = [
                    values[p][w][at : at + 1, 128 * c : 128 * (c + 1)] for w in range(2) for c in range(4)
                ]
                corner_out[r, m, n] = jnp.concatenate(rows, axis=0)
        for present, up, down in sides[2:]:
            @pl.when(present)
            def _(up=up, down=down):
                halo_copy(r, up, down).start()

    def held_copy(n, batch):
        return pltpu.make_async_remote_copy(
            src_ref=planes.at[pl.ds(4 * batch + 1, 4), n],
            dst_ref=held.at[pl.ds(4 * batch, 4), wide],
            send_sem=held_send.at[batch, n],
            recv_sem=held_recv.at[batch, wide],
            device_id=plane_at(n),
            device_id_type=MESH,
        )

    initial = [[field[0, p + 2, w, pl.ds(0, WIDE), :] for w in range(2)] for p in range(DEEP)]
    for p in range(DEEP):
        publish(0, p, initial[p])
    send(0, initial)

    for n, p, row in ((0, 0, 0), (1, DEEP - 1, WIDE - 1)):
        for w in range(2):
            first_z[n, w] = field[1, p + 2, w, pl.ds(0, WIDE), :]
            for q in range(DEEP):
                first_y[n, pl.ds(DEEP * w + q, 1), :] = field[1, q + 2, w, pl.ds(row, 1), :]
        first_z[n, 2] = cour[p + 1, pl.ds(0, WIDE), :]
        for q in range(DEEP):
            first_y[n, pl.ds(2 * DEEP + q, 1), :] = cour[q + 1, pl.ds(row, 1), :]
        first_y[n, pl.ds(3 * DEEP, DEEP), :] = jnp.zeros((DEEP, COLS), F32)
    for present, up, down in sides[:4]:
        @pl.when(present)
        def _(up=up, down=down):
            first_copy(up, down).start()

    for present, up, down in sides[:4]:
        @pl.when(present)
        def _(up=up, down=down):
            first_copy(-up, -down).wait_recv()
            if up:
                there, at = (first_hi, DEEP + 2) if up > 0 else (first_lo, 1)
                for w in range(2):
                    field[1, at, w, pl.ds(0, WIDE), :] = there[w]
                cour[at - 1, pl.ds(0, WIDE), :] = there[2]
            else:
                n, at = (0, WIDE) if down > 0 else (1, RING - 1)
                for q in range(DEEP):
                    for w in range(2):
                        field[1, q + 2, w, pl.ds(at, 1), :] = first_in[n, pl.ds(DEEP * w + q, 1), :]
                    cour[q + 1, pl.ds(at, 1), :] = first_in[n, pl.ds(2 * DEEP + q, 1), :]

    row_id = lax.broadcasted_iota(jnp.int32, (RING, COLS), 0)
    col_id = lax.broadcasted_iota(jnp.int32, (RING, COLS), 1)
    source = src_ref[0]
    source_row = ((source >> 9) & (NY - 1)) - first_row
    source_row = jnp.where((source_row >= -1) & (source_row <= WIDE), source_row & (RING - 1), -1)
    source_plane = (source >> 16) - first_plane + 2
    at_source = (row_id == source_row) & (col_id == (source & (COLS - 1)))

    def step(t, now, p, w, height):
        u = field[now, p, w]
        beside = pltpu.roll(u, 1, 0)[:height] + pltpu.roll(u, RING - 1, 0)[:height]
        u = u[:height]
        beside += field[now, p - 1, w, pl.ds(0, height), :] + field[now, p + 1, w, pl.ds(0, height), :]
        col = col_id[:height]
        beside += jnp.where(col == 0, 0.0, pltpu.roll(u, 1, 1))
        beside += jnp.where(col == COLS - 1, 0.0, pltpu.roll(u, COLS - 1, 1))
        if w == 1:
            injection = inj[t, p - 1, pl.ds(0, height), :]
        else:
            injection = jnp.where(at_source[:height] & (source_plane == p), wav_ref[t], 0.0)
        before = field[1 - now, p, w, pl.ds(0, height), :]
        following = 2.0 * u - before + cour[p - 1, pl.ds(0, height), :] * (beside - 6.0 * u) + injection
        field[1 - now, p, w, pl.ds(0, height), :] = following
        return following

    def advance(r, carry):
        for i in range(EACH):
            k = AHEAD + EACH * r + i

            @pl.when(k < BESIDE)
            def _(k=k):
                send_spectra(k)

        lax.fori_loop(2 * r, 2 * r + 2, inject, 0)
        share = terms // ROUNDS
        lax.fori_loop(share * r, share * (r + 1), fill, 0)

        for present, up, down in sides:
            @pl.when(present)
            def _(up=up, down=down):
                halo_copy(r, -up, -down).wait_recv()
                if not down:
                    there, at = (hi, DEEP + 2) if up > 0 else (lo, 0)
                    for q in range(2):
                        both = there[r, q].astype(F32)
                        for w in range(2):
                            field[0, at + q, w, pl.ds(0, WIDE), :] = both[WIDE * w : WIDE * (w + 1)]
                    return
                n, at = (0, WIDE) if down > 0 else (1, RING - 2)
                if not up:
                    rows = yin[r, n].astype(F32)
                    for p in range(DEEP):
                        for w in range(2):
                            i = 4 * p + 2 * w
                            field[0, p + 2, w, pl.ds(at, 2), :] = rows[i : i + 2]
                else:
                    m, q = (0, DEEP + 2) if up > 0 else (1, 1)
                    at = WIDE if down > 0 else RING - 1
                    for w in range(2):
                        for c in range(4):
                            field[0, q, w, pl.ds(at, 1), pl.ds(128 * c, 128)] = corner[
                                r, m, n, pl.ds(4 * w + c, 1), :
                            ]

        t = 2 * r
        middle = [
            [step(t, 0, p, w, RING if 1 < p < DEEP + 2 else WIDE) for w in range(2)]
            for p in range(1, DEEP + 3)
        ]
        last = [[step(t + 1, 1, p, w, WIDE) for w in range(2)] for p in range(2, DEEP + 2)]
        for p in range(DEEP):
            publish(t + 2, p, last[p])

        @pl.when(r < ROUNDS - 1)
        def _():
            send(r + 1, last)

        for p in range(DEEP):
            publish(t + 1, p, [values[:WIDE] for values in middle[p + 1]])

        @pl.when(owns)
        def _():
            for i in (1, 2):
                held[t + i - 1, wide] = planes[t + i, post]

        for n in range(4):
            @pl.when((r % 2 == 1) & jnp.logical_not(owns & (post == n)))
            def _(n=n):
                held_copy(n, r // 2).start()

        return carry

    lax.fori_loop(0, ROUNDS, advance, 0)

    def rest(k, carry):
        send_spectra(k)
        return carry

    lax.fori_loop(BESIDE, TERMS, rest, 0)

    def turn_batch(batch, carry):
        for n in range(4):
            @pl.when(jnp.logical_not(owns & (post == n)))
            def _(n=n):
                pltpu.make_async_remote_copy(
                    src_ref=planes.at[pl.ds(4 * batch + 1, 4), n],
                    dst_ref=held.at[pl.ds(4 * batch, 4), swung(f, n)],
                    send_sem=held_send.at[batch, n], recv_sem=held_recv.at[batch, swung(f, n)],
                    device_id=plane_at(n), device_id_type=MESH,
                ).wait_recv()

        def turn(q, inner):
            t = 4 * batch + q
            strips = held[t].astype(F32)
            for w in range(2):
                plane = turned(strips[:, WIDE * w : WIDE * (w + 1)].reshape(ROWS, COLS)).astype(BF16)
                for i in range(XS // HALF):
                    snaps[w, i // 2, t, :, pl.ds((i % 2) * XS, XS)] = plane[HALF * i : HALF * (i + 1)]
            return inner

        return lax.fori_loop(0, 4, turn, carry)

    lax.fori_loop(0, STEPS // 4, turn_batch, 0)

    offsets = [2 * lag_ref[h] + 2 * LAGMAX for h in range(lags)]
    batch = ROUND * NF

    def clear(h, carry):
        sums[h] = jnp.zeros(sums.shape[1:], F32)
        return carry

    lax.fori_loop(0, lags, clear, 0)

    def one_round(r, carry):
        def arrive(q, inner):
            k = r * ROUND + q
            for o in range(NF - 1):
                pltpu.make_async_remote_copy(
                    src_ref=outgoing.at[o, k], dst_ref=fresh.at[peers[o], k],
                    send_sem=spec_send.at[o, k], recv_sem=spec_recv.at[peers[o], k],
                    device_id=group_at(peers[o]), device_id_type=MESH,
                ).wait_recv()
            return inner

        lax.fori_loop(0, ROUND, arrive, 0)
        size = batch * HALF
        table = mix[pl.ds(pl.multiple_of(r * size, size), size), :]
        for w in range(2):
            for pair in range(XS // HALF // 2):
                moments = snaps[w, pair].reshape(STEPS * HALF, 2 * XS)
                part = jnp.dot(table, moments, preferred_element_type=F32).reshape(batch, HALF, 2 * XS)
                for q in range(ROUND):
                    for g in range(NF):
                        for i in range(2):
                            at = HALF * (2 * pair + i)
                            total = part[q * NF + g, :, XS * i : XS * (i + 1)]
                            total += fresh[g, r * ROUND + q, w, pl.ds(at, HALF), :].astype(F32)
                            if w == 0:
                                early[q * NF + g, pl.ds(at, HALF), :] = total
                            else:
                                late[q * NF + g, pl.ds(at + 2 * LAGMAX, HALF), :] = total

        def wrap(k, inner):
            late[k, pl.ds(0, 2 * LAGMAX), :] = pltpu.roll(late[k, pl.ds(XS, 2 * LAGMAX), :], ROWS, 1)
            late[k, pl.ds(XS + 2 * LAGMAX, 2 * LAGMAX), :] = pltpu.roll(
                late[k, pl.ds(2 * LAGMAX, 2 * LAGMAX), :], XS - ROWS, 1
            )
            return inner

        lax.fori_loop(0, batch, wrap, 0)

        def tile(i, inner):
            at = pl.multiple_of(i * HALF, HALF)
            starts = [at + offset for offset in offsets]

            def add(k, totals):
                for step in range(4):
                    one = early[4 * k + step, pl.ds(at, HALF), :]
                    totals = tuple(
                        total + one * late[4 * k + step, pl.ds(start, HALF), :]
                        for total, start in zip(totals, starts)
                    )
                return totals

            totals = lax.fori_loop(
                0, batch // 4, add, tuple(sums[h, pl.ds(at + LAGMAX, HALF), :] for h in range(lags))
            )
            for h in range(lags):
                sums[h, pl.ds(at + LAGMAX, HALF), :] = totals[h]
            return inner

        return lax.fori_loop(0, XS // HALF, tile, carry)

    lax.fori_loop(0, TERMS // ROUND, one_round, 0)

    x = (
        lax.broadcasted_iota(jnp.int32, (XS, XS), 0)
        + lax.broadcasted_iota(jnp.int32, (XS, XS), 1) // ROWS * XS
    )
    weight = 1.0 / (STEPS * terms / 2)

    def finish(h, carry):
        lag = lag_ref[h]
        sums[h, pl.ds(0, LAGMAX), :] = pltpu.roll(sums[h, pl.ds(XS, LAGMAX), :], ROWS, 1)
        sums[h, pl.ds(XS + LAGMAX, LAGMAX), :] = pltpu.roll(sums[h, pl.ds(LAGMAX, LAGMAX), :], XS - ROWS, 1)
        moved = sums[h, pl.ds(LAGMAX - lag, XS), :]
        reach = jnp.abs(lag)
        kept = jnp.where((x >= reach) & (x < COLS - reach), moved * weight, 0.0).T
        for c in range(BLOCKS):
            out[h, :, pl.ds(XS * c, XS)] = kept[ROWS * c : ROWS * (c + 1)].astype(BF16)
        return carry

    lax.fori_loop(0, lags, finish, 0)

    def sent(r, carry):
        for present, up, down in sides:
            @pl.when(present)
            def _(up=up, down=down):
                halo_copy(r, up, down).wait_send()

        return carry

    lax.fori_loop(0, ROUNDS, sent, 0)

    for present, up, down in sides[:4]:
        @pl.when(present)
        def _(up=up, down=down):
            first_copy(up, down).wait_send()

    def spectra_sent(k, carry):
        for o in range(NF - 1):
            spec_copy(o, k).wait_send()
        return carry

    lax.fori_loop(0, TERMS, spectra_sent, 0)

    def delivered(batch, carry):
        for n in range(4):
            @pl.when(jnp.logical_not(owns & (post == n)))
            def _(n=n):
                held_copy(n, batch).wait_send()

        return carry

    lax.fori_loop(0, STEPS // 4, delivered, 0)

    for n in range(4):
        @pl.when(home != n)
        def _(n=n):
            relay_copy(n).wait_send()

        @pl.when(jnp.logical_not(mine & (f == n)))
        def _(n=n):
            piece_copy(n).wait_send()


def body(
    previous_field, current_field, courant, wavelet, traces, source_cell, receiver_cells,
    frequency_list, lag_list, spectra,
):
    lags, terms = lag_list.shape[0], NF * TERMS
    table = dft_table(frequency_list).reshape(STEPS, NF, TERMS).transpose(2, 1, 0).reshape(terms, STEPS)
    vmem = pl.BlockSpec(memory_space=pltpu.VMEM)
    smem = pl.BlockSpec(memory_space=pltpu.SMEM)
    dma = pltpu.SemaphoreType.DMA
    pair = (2 * WIDE, COLS)
    image = pl.pallas_call(
        kernel,
        out_shape=jax.ShapeDtypeStruct((lags, ROWS, COLS), BF16),
        in_specs=[vmem, vmem, vmem, smem, vmem, smem, vmem, smem, vmem, pl.BlockSpec(memory_space=pl.ANY)],
        out_specs=vmem,
        scratch_shapes=[
            pltpu.VMEM((NF, 2, TERMS, ROWS, COLS), F32),
            pltpu.VMEM((NF - 1, TERMS, 2, XS, XS), BF16),
            pltpu.VMEM((NF, TERMS, 2, XS, XS), BF16),
            pltpu.VMEM((4, 5, DEEP * WIDE, 128), BF16),
            pltpu.VMEM((4, 5, DEEP * WIDE, 128), BF16),
            pltpu.VMEM((NF, 5, DEEP * WIDE, 128), BF16),
            pltpu.VMEM((2, DEEP + 4, 2, RING, COLS), F32),
            pltpu.VMEM((DEEP + 2, RING, COLS), F32),
            pltpu.VMEM((STEPS, DEEP + 2, RING, COLS), F32),
            pltpu.VMEM((STEPS + 1, DEEP) + pair, BF16),
            pltpu.VMEM((STEPS, 4) + pair, BF16),
            pltpu.VMEM((ROUNDS, 2) + pair, BF16),
            pltpu.VMEM((ROUNDS, 2) + pair, BF16),
            pltpu.VMEM((ROUNDS, 2, 4 * DEEP, COLS), BF16),
            pltpu.VMEM((ROUNDS, 2, 4 * DEEP, COLS), BF16),
            pltpu.VMEM((ROUNDS, 2, 2, 8, 128), F32),
            pltpu.VMEM((ROUNDS, 2, 2, 8, 128), F32),
            pltpu.VMEM((2, 3, WIDE, COLS), F32),
            pltpu.VMEM((2, 4 * DEEP, COLS), F32),
            pltpu.VMEM((3, WIDE, COLS), F32),
            pltpu.VMEM((3, WIDE, COLS), F32),
            pltpu.VMEM((2, 4 * DEEP, COLS), F32),
            pltpu.VMEM((terms, STEPS * HALF), F32),
            pltpu.VMEM((terms * HALF, STEPS * HALF), BF16),
            pltpu.VMEM((2, XS // HALF // 2, STEPS, HALF, 2 * XS), BF16),
            pltpu.VMEM((ROUND * NF, XS, XS), F32),
            pltpu.VMEM((ROUND * NF, XS + 4 * LAGMAX, XS), F32),
            pltpu.VMEM((lags, XS + 2 * LAGMAX, XS), F32),
            dma((NF, 2)),
            dma((NF - 1, TERMS)),
            dma((NF, TERMS)),
            dma((4,)),
            dma((4,)),
            dma((4,)),
            dma((NF,)),
            dma((ROUNDS, 2)),
            dma((ROUNDS, 2)),
            dma((ROUNDS, 2)),
            dma((ROUNDS, 2)),
            dma((ROUNDS, 4)),
            dma((ROUNDS, 4)),
            dma((4,)),
            dma((4,)),
            dma((STEPS // 4, 4)),
            dma((STEPS // 4, 4)),
        ],
        compiler_params=pltpu.CompilerParams(
            collective_id=0, has_side_effects=True, vmem_limit_bytes=56 * 2**20
        ),
        name="window_image",
    )(
        previous_field, current_field, courant, wavelet, traces, source_cell,
        receiver_cells.reshape(1, -1), lag_list, table, spectra.reshape(2, TERMS, NY, COLS),
    )
    return image.reshape(lags, 1, 1, ROWS, COLS)


def solution(mesh):
    placed = (
        P(None, "xy", "slab", "freq"),
        P(None, "xy", "slab", "freq"),
        P("xy", "slab", "freq"),
        P(),
        P(),
        P(),
        P(),
        P(),
        P(),
        P(None, "freq", None, "xy", "slab", None, None),
    )
    return jax.shard_map(
        body,
        mesh=mesh,
        in_specs=placed,
        out_specs=P(None, "xy", "slab", "freq", None),
        check_vma=False,
    )
```

```python
import math

import jax
import jax.numpy as jnp
from jax import lax
from jax.experimental import pallas as pl
from jax.experimental.pallas import tpu as pltpu
from jax.sharding import PartitionSpec as P

STEPS = 16
NTOT = 2048
LAGMAX = 16
NF, NS, NB = 4, 16, 4
ROWS, COLS = 32, 512
DEEP, WIDE = 4, 8
RING = 16
TERMS = 16
NY = NF * ROWS
F32, BF16 = jnp.float32, jnp.bfloat16
XS = 128
BLOCKS = COLS // XS
HALF = 16
ROUND = 2
ROUNDS = STEPS // 2
AHEAD, EACH, BESIDE = 1, 1, 9
MESH = pl.DeviceIdType.MESH


def dft_table(frequency_list):
    moments = jnp.arange(STEPS, dtype=jnp.int32) + (NTOT - STEPS)
    phase_index = moments[:, None] * frequency_list[None, :] % NTOT
    phase_angle = phase_index.astype(F32) * (2.0 * math.pi / NTOT)
    return jnp.stack([jnp.cos(phase_angle), -jnp.sin(phase_angle)], axis=-1).astype(BF16)


def swung(outer, inner):
    return inner + outer % 2 * (3 - 2 * inner)


def turned(rows):
    return jnp.concatenate([rows[:, XS * c : XS * (c + 1)] for c in range(BLOCKS)], axis=0).T


def kernel(
    prev_ref, cur_ref, cour_ref, wav_ref, traces_ref, src_ref, rec_ref, lag_ref, table_ref, spec_ref,
    out,
    raw, outgoing, fresh, pieces_out, relay, pieces_in, field, cour, inj, planes, held, lo, hi, yout, yin, corner_out, corner, first_z, first_y, first_lo, first_hi, first_in,
    spread, mix, snaps, early, late, sums,
    raw_sem, spec_send, spec_recv, relay_send, relay_recv, piece_send, piece_recv,
    zsend, zrecv, ysend, yrecv, csend, crecv, fsend, frecv, held_send, held_recv,
):
    f, j, b = lax.axis_index("freq"), lax.axis_index("slab"), lax.axis_index("xy")
    home, post = j // 4, j % 4
    deep, wide = swung(b, home), swung(f, post)
    layer, strip = b * 4 + deep, f * 4 + wide
    first_plane, first_row = layer * DEEP, strip * WIDE
    has_lo, has_hi = layer > 0, layer < NB * 4 - 1
    has_top, has_bottom = strip > 0, strip < NF * 4 - 1
    lags = lag_ref.shape[0]

    def block_at(up, down):
        to_layer, to_strip = layer + up, strip + down
        return {
            "freq": to_strip // 4,
            "slab": swung(to_layer // 4, to_layer % 4) * 4 + swung(to_strip // 4, to_strip % 4),
            "xy": to_layer // 4,
        }

    def group_at(other):
        return {"freq": other, "slab": j, "xy": b}

    def plane_at(other):
        return {"freq": f, "slab": deep * 4 + other, "xy": b}

    peers = (lax.rem(f + 2, NF), NF - 1 - f, f + 1 - 2 * lax.rem(f, 2))
    chunk = peers + (f,)
    owns = b % 2 == 0

    def raw_copy(o, w):
        return pltpu.make_async_copy(
            spec_ref.at[w, :, pl.ds(chunk[o] * ROWS, ROWS), :], raw.at[o, w], raw_sem.at[o, w]
        )

    for o in range(NF):
        for w in range(2):
            raw_copy(o, w).start()

    barrier = pltpu.get_barrier_semaphore()
    mine = f % 2 == 0

    def greet(there):
        pl.semaphore_signal(barrier, 1, device_id=there, device_id_type=MESH)

    for p in peers:
        greet(group_at(p))
    for n in range(4):
        @pl.when(jnp.logical_not(owns & (post == n)))
        def _(n=n):
            greet(plane_at(n))

    sides = (
        (has_hi, 1, 0), (has_lo, -1, 0), (has_bottom, 0, 1), (has_top, 0, -1),
        (has_hi & has_bottom, 1, 1), (has_hi & has_top, 1, -1),
        (has_lo & has_bottom, -1, 1), (has_lo & has_top, -1, -1),
    )
    for present, up, down in sides:
        @pl.when(present)
        def _(up=up, down=down):
            greet(block_at(up, down))

    for n in range(4):
        @pl.when(home != n)
        def _(n=n):
            greet({"freq": f, "slab": 4 * n + post, "xy": b})

    for f0 in range(NF):
        @pl.when(jnp.logical_not(mine & (f == f0)))
        def _(f0=f0):
            greet({"freq": f0, "slab": 4 * home + wide, "xy": b})

    def stack(group, carry):
        at = pl.ds(group * DEEP, DEEP)
        for w in range(2):
            pieces_out[group, w] = prev_ref[w, at].reshape(DEEP * WIDE, 128).astype(BF16)
            pieces_out[group, 2 + w] = cur_ref[w, at].reshape(DEEP * WIDE, 128).astype(BF16)
        exact = cour_ref[at].reshape(DEEP * WIDE, 128)
        rounded = exact.astype(BF16)
        pieces_out[group, 4] = rounded
        pieces_out[group, 5] = (exact - rounded.astype(F32)).astype(BF16)
        return carry

    lax.fori_loop(0, 4, stack, 0)

    expected = len(peers) + 4 + 3 + NF - mine.astype(jnp.int32) - owns.astype(jnp.int32)
    for present, _, _ in sides:
        expected += present.astype(jnp.int32)
    pl.semaphore_wait(barrier, expected)

    def relay_copy(n):
        group = swung(b, n)
        return pltpu.make_async_remote_copy(
            src_ref=pieces_out.at[group],
            dst_ref=relay.at[home],
            send_sem=relay_send.at[n],
            recv_sem=relay_recv.at[home],
            device_id={"freq": f, "slab": 4 * n + post, "xy": b},
            device_id_type=MESH,
        )

    def piece_copy(n):
        return pltpu.make_async_remote_copy(
            src_ref=relay.at[n],
            dst_ref=pieces_in.at[f],
            send_sem=piece_send.at[n],
            recv_sem=piece_recv.at[f],
            device_id={"freq": n, "slab": 4 * home + swung(n, post), "xy": b},
            device_id_type=MESH,
        )

    for n in range(4):
        @pl.when(home != n)
        def _(n=n):
            relay_copy(n).start()

    relay[home] = pieces_out[deep]

    for n in range(4):
        @pl.when(home != n)
        def _(n=n):
            pltpu.make_async_remote_copy(
                src_ref=pieces_out.at[n], dst_ref=relay.at[n],
                send_sem=relay_send.at[n], recv_sem=relay_recv.at[n],
                device_id={"freq": f, "slab": 4 * n + post, "xy": b}, device_id_type=MESH,
            ).wait_recv()

        @pl.when(jnp.logical_not(mine & (f == n)))
        def _(n=n):
            piece_copy(n).start()

    @pl.when(mine)
    def _():
        pieces_in[f] = relay[f]

    def spec_copy(o, k):
        return pltpu.make_async_remote_copy(
            src_ref=outgoing.at[o, k],
            dst_ref=fresh.at[f, k],
            send_sem=spec_send.at[o, k],
            recv_sem=spec_recv.at[f, k],
            device_id=group_at(peers[o]),
            device_id_type=MESH,
        )

    def send_spectra(k):
        for o in range(NF - 1):
            for w in range(2):
                outgoing[o, k, w] = turned(raw[o, w, k]).astype(BF16)
            spec_copy(o, k).start()
        for w in range(2):
            fresh[f, k, w] = turned(raw[NF - 1, w, k]).astype(BF16)

    for o in range(NF):
        for w in range(2):
            raw_copy(o, w).wait()

    for k in range(AHEAD):
        send_spectra(k)

    cell = rec_ref[...]
    depth, row, col = (cell >> 16) - first_plane + 1, ((cell >> 9) & (NY - 1)) - first_row, cell & (COLS - 1)
    here = (depth >= 0) & (depth < DEEP + 2) & (row >= -1) & (row <= WIDE)
    row = jnp.where(here, depth * RING + (row & (RING - 1)), -1)
    size = (DEEP + 2) * RING
    at_row = lax.broadcasted_iota(jnp.int32, (size, cell.shape[1]), 0) == row
    at_col = (lax.broadcasted_iota(jnp.int32, (COLS, cell.shape[1]), 0) == col).astype(F32).astype(BF16)

    def inject(t, carry):
        values = jnp.where(at_row, traces_ref[pl.ds(t, 1), :], 0.0)
        first = values.astype(BF16)
        rest = values - first.astype(F32)
        second = rest.astype(BF16)
        third = (rest - second.astype(F32)).astype(BF16)
        parts = lax.dot_general(
            jnp.concatenate([first, second, third], axis=0), at_col,
            (((1,), (1,)), ((), ())), preferred_element_type=F32,
        )
        total = parts[:size] + parts[size : 2 * size] + parts[2 * size :]
        inj[t] = total.reshape(DEEP + 2, RING, COLS)
        return carry

    terms = NF * TERMS
    step_of = lax.broadcasted_iota(jnp.int32, (STEPS, STEPS * HALF), 1) // HALF
    chosen = (step_of == lax.broadcasted_iota(jnp.int32, (STEPS, STEPS * HALF), 0)).astype(F32).astype(BF16)
    spread[...] = jnp.dot(table_ref[...], chosen, preferred_element_type=F32)
    place = lax.broadcasted_iota(jnp.int32, (HALF, STEPS * HALF), 1) % HALF
    diagonal = place == lax.broadcasted_iota(jnp.int32, (HALF, STEPS * HALF), 0)

    def fill(k, carry):
        values = jnp.where(diagonal, spread[pl.ds(k, 1), :], 0.0)
        mix[pl.ds(pl.multiple_of(k * HALF, HALF), HALF), :] = values.astype(BF16)
        return carry

    def clear_plane(p, carry):
        for n in range(2):
            for w in range(2):
                field[n, p, w] = jnp.zeros((RING, COLS), F32)

        @pl.when(p < DEEP + 2)
        def _():
            cour[p] = jnp.zeros((RING, COLS), F32)

        return carry

    lax.fori_loop(0, DEEP + 4, clear_plane, 0)

    for f0 in range(NF):
        @pl.when(jnp.logical_not(mine & (f == f0)))
        def _(f0=f0):
            pltpu.make_async_remote_copy(
                src_ref=pieces_out.at[0], dst_ref=pieces_in.at[f0],
                send_sem=piece_send.at[0], recv_sem=piece_recv.at[f0],
                device_id=group_at(f), device_id_type=MESH,
            ).wait_recv()

        cols = pl.ds(128 * f0, 128)
        piece = [pieces_in[f0, n].astype(F32) for n in range(6)]
        for p in range(DEEP):
            rows = slice(WIDE * p, WIDE * (p + 1))
            for w in range(2):
                field[1, p + 2, w, pl.ds(0, WIDE), cols] = piece[w][rows]
                field[0, p + 2, w, pl.ds(0, WIDE), cols] = piece[2 + w][rows]
            cour[p + 1, pl.ds(0, WIDE), cols] = piece[4][rows] + piece[5][rows]

    def halo_copy(r, up, down):
        if not down:
            low = up > 0
            src, dst = planes.at[2 * r, pl.ds(DEEP - 2 if low else 0, 2)], (lo if low else hi).at[r]
            sems = zsend.at[r, int(low)], zrecv.at[r, int(low)]
        elif not up:
            n = int(down > 0)
            src, dst, sems = yout.at[r, n], yin.at[r, n], (ysend.at[r, n], yrecv.at[r, n])
        else:
            n, m = int(down > 0), int(up > 0)
            src, dst = corner_out.at[r, m, n], corner.at[r, m, n]
            sems = csend.at[r, 2 * m + n], crecv.at[r, 2 * m + n]
        return pltpu.make_async_remote_copy(
            src_ref=src, dst_ref=dst, send_sem=sems[0], recv_sem=sems[1],
            device_id=block_at(up, down), device_id_type=MESH,
        )

    def first_copy(up, down):
        n = int(up + down > 0)
        if up:
            src, dst, m = first_z.at[n], (first_lo if n else first_hi), n
        else:
            src, dst, m = first_y.at[n], first_in.at[n], 2 + n
        return pltpu.make_async_remote_copy(
            src_ref=src, dst_ref=dst, send_sem=fsend.at[m], recv_sem=frecv.at[m],
            device_id=block_at(up, down), device_id_type=MESH,
        )

    def publish(s, p, values):
        planes[s, p] = jnp.concatenate(values, axis=0).astype(BF16)

    def send(r, values):
        for present, up, down in sides[:2]:
            @pl.when(present)
            def _(up=up, down=down):
                halo_copy(r, up, down).start()

        for n, at in ((0, 0), (1, WIDE - 2)):
            rows = [values[p][w][at : at + 2] for p in range(DEEP) for w in range(2)]
            yout[r, n] = jnp.concatenate(rows, axis=0).astype(BF16)
        for m, p in ((0, 0), (1, DEEP - 1)):
            for n, at in ((0, 0), (1, WIDE - 1)):
                rows = [
                    values[p][w][at : at + 1, 128 * c : 128 * (c + 1)] for w in range(2) for c in range(4)
                ]
                corner_out[r, m, n] = jnp.concatenate(rows, axis=0)
        for present, up, down in sides[2:]:
            @pl.when(present)
            def _(up=up, down=down):
                halo_copy(r, up, down).start()

    def held_copy(n, batch):
        return pltpu.make_async_remote_copy(
            src_ref=planes.at[pl.ds(4 * batch + 1, 4), n],
            dst_ref=held.at[pl.ds(4 * batch, 4), wide],
            send_sem=held_send.at[batch, n],
            recv_sem=held_recv.at[batch, wide],
            device_id=plane_at(n),
            device_id_type=MESH,
        )

    initial = [[field[0, p + 2, w, pl.ds(0, WIDE), :] for w in range(2)] for p in range(DEEP)]
    for p in range(DEEP):
        publish(0, p, initial[p])
    send(0, initial)

    for n, p, row in ((0, 0, 0), (1, DEEP - 1, WIDE - 1)):
        for w in range(2):
            first_z[n, w] = field[1, p + 2, w, pl.ds(0, WIDE), :]
            for q in range(DEEP):
                first_y[n, pl.ds(DEEP * w + q, 1), :] = field[1, q + 2, w, pl.ds(row, 1), :]
        first_z[n, 2] = cour[p + 1, pl.ds(0, WIDE), :]
        for q in range(DEEP):
            first_y[n, pl.ds(2 * DEEP + q, 1), :] = cour[q + 1, pl.ds(row, 1), :]
        first_y[n, pl.ds(3 * DEEP, DEEP), :] = jnp.zeros((DEEP, COLS), F32)
    for present, up, down in sides[:4]:
        @pl.when(present)
        def _(up=up, down=down):
            first_copy(up, down).start()

    for present, up, down in sides[:4]:
        @pl.when(present)
        def _(up=up, down=down):
            first_copy(-up, -down).wait_recv()
            if up:
                there, at = (first_hi, DEEP + 2) if up > 0 else (first_lo, 1)
                for w in range(2):
                    field[1, at, w, pl.ds(0, WIDE), :] = there[w]
                cour[at - 1, pl.ds(0, WIDE), :] = there[2]
            else:
                n, at = (0, WIDE) if down > 0 else (1, RING - 1)
                for q in range(DEEP):
                    for w in range(2):
                        field[1, q + 2, w, pl.ds(at, 1), :] = first_in[n, pl.ds(DEEP * w + q, 1), :]
                    cour[q + 1, pl.ds(at, 1), :] = first_in[n, pl.ds(2 * DEEP + q, 1), :]

    row_id = lax.broadcasted_iota(jnp.int32, (RING, COLS), 0)
    col_id = lax.broadcasted_iota(jnp.int32, (RING, COLS), 1)
    source = src_ref[0]
    source_row = ((source >> 9) & (NY - 1)) - first_row
    source_row = jnp.where((source_row >= -1) & (source_row <= WIDE), source_row & (RING - 1), -1)
    source_plane = (source >> 16) - first_plane + 2
    at_source = (row_id == source_row) & (col_id == (source & (COLS - 1)))

    def step(t, now, p, w, height):
        u = field[now, p, w]
        beside = pltpu.roll(u, 1, 0)[:height] + pltpu.roll(u, RING - 1, 0)[:height]
        u = u[:height]
        beside += field[now, p - 1, w, pl.ds(0, height), :] + field[now, p + 1, w, pl.ds(0, height), :]
        col = col_id[:height]
        beside += jnp.where(col == 0, 0.0, pltpu.roll(u, 1, 1))
        beside += jnp.where(col == COLS - 1, 0.0, pltpu.roll(u, COLS - 1, 1))
        if w == 1:
            injection = inj[t, p - 1, pl.ds(0, height), :]
        else:
            injection = jnp.where(at_source[:height] & (source_plane == p), wav_ref[t], 0.0)
        before = field[1 - now, p, w, pl.ds(0, height), :]
        following = 2.0 * u - before + cour[p - 1, pl.ds(0, height), :] * (beside - 6.0 * u) + injection
        field[1 - now, p, w, pl.ds(0, height), :] = following
        return following

    def advance(r, carry):
        for i in range(EACH):
            k = AHEAD + EACH * r + i

            @pl.when(k < BESIDE)
            def _(k=k):
                send_spectra(k)

        lax.fori_loop(2 * r, 2 * r + 2, inject, 0)
        share = terms // ROUNDS
        lax.fori_loop(share * r, share * (r + 1), fill, 0)

        for present, up, down in sides:
            @pl.when(present)
            def _(up=up, down=down):
                halo_copy(r, -up, -down).wait_recv()
                if not down:
                    there, at = (hi, DEEP + 2) if up > 0 else (lo, 0)
                    for q in range(2):
                        both = there[r, q].astype(F32)
                        for w in range(2):
                            field[0, at + q, w, pl.ds(0, WIDE), :] = both[WIDE * w : WIDE * (w + 1)]
                    return
                n, at = (0, WIDE) if down > 0 else (1, RING - 2)
                if not up:
                    rows = yin[r, n].astype(F32)
                    for p in range(DEEP):
                        for w in range(2):
                            i = 4 * p + 2 * w
                            field[0, p + 2, w, pl.ds(at, 2), :] = rows[i : i + 2]
                else:
                    m, q = (0, DEEP + 2) if up > 0 else (1, 1)
                    at = WIDE if down > 0 else RING - 1
                    for w in range(2):
                        for c in range(4):
                            field[0, q, w, pl.ds(at, 1), pl.ds(128 * c, 128)] = corner[
                                r, m, n, pl.ds(4 * w + c, 1), :
                            ]

        t = 2 * r
        middle = [
            [step(t, 0, p, w, RING if 1 < p < DEEP + 2 else WIDE) for w in range(2)]
            for p in range(1, DEEP + 3)
        ]
        last = [[step(t + 1, 1, p, w, WIDE) for w in range(2)] for p in range(2, DEEP + 2)]
        for p in range(DEEP):
            publish(t + 2, p, last[p])

        @pl.when(r < ROUNDS - 1)
        def _():
            send(r + 1, last)

        for p in range(DEEP):
            publish(t + 1, p, [values[:WIDE] for values in middle[p + 1]])

        @pl.when(owns)
        def _():
            for i in (1, 2):
                held[t + i - 1, wide] = planes[t + i, post]

        for n in range(4):
            @pl.when((r % 2 == 1) & jnp.logical_not(owns & (post == n)))
            def _(n=n):
                held_copy(n, r // 2).start()

        return carry

    lax.fori_loop(0, ROUNDS, advance, 0)

    def rest(k, carry):
        send_spectra(k)
        return carry

    lax.fori_loop(BESIDE, TERMS, rest, 0)

    def turn_batch(batch, carry):
        for n in range(4):
            @pl.when(jnp.logical_not(owns & (post == n)))
            def _(n=n):
                pltpu.make_async_remote_copy(
                    src_ref=planes.at[pl.ds(4 * batch + 1, 4), n],
                    dst_ref=held.at[pl.ds(4 * batch, 4), swung(f, n)],
                    send_sem=held_send.at[batch, n], recv_sem=held_recv.at[batch, swung(f, n)],
                    device_id=plane_at(n), device_id_type=MESH,
                ).wait_recv()

        def turn(q, inner):
            t = 4 * batch + q
            strips = held[t].astype(F32)
            for w in range(2):
                plane = turned(strips[:, WIDE * w : WIDE * (w + 1)].reshape(ROWS, COLS)).astype(BF16)
                for i in range(XS // HALF):
                    snaps[w, i // 2, t, :, pl.ds((i % 2) * XS, XS)] = plane[HALF * i : HALF * (i + 1)]
            return inner

        return lax.fori_loop(0, 4, turn, carry)

    lax.fori_loop(0, STEPS // 4, turn_batch, 0)

    offsets = [2 * lag_ref[h] + 2 * LAGMAX for h in range(lags)]
    batch = ROUND * NF

    def clear(h, carry):
        sums[h] = jnp.zeros(sums.shape[1:], F32)
        return carry

    lax.fori_loop(0, lags, clear, 0)

    def one_round(r, carry):
        def arrive(q, inner):
            k = r * ROUND + q
            for o in range(NF - 1):
                pltpu.make_async_remote_copy(
                    src_ref=outgoing.at[o, k], dst_ref=fresh.at[peers[o], k],
                    send_sem=spec_send.at[o, k], recv_sem=spec_recv.at[peers[o], k],
                    device_id=group_at(peers[o]), device_id_type=MESH,
                ).wait_recv()
            return inner

        lax.fori_loop(0, ROUND, arrive, 0)
        size = batch * HALF
        table = mix[pl.ds(pl.multiple_of(r * size, size), size), :]
        for w in range(2):
            for pair in range(XS // HALF // 2):
                moments = snaps[w, pair].reshape(STEPS * HALF, 2 * XS)
                part = jnp.dot(table, moments, preferred_element_type=F32).reshape(batch, HALF, 2 * XS)
                for q in range(ROUND):
                    for g in range(NF):
                        for i in range(2):
                            at = HALF * (2 * pair + i)
                            total = part[q * NF + g, :, XS * i : XS * (i + 1)]
                            total += fresh[g, r * ROUND + q, w, pl.ds(at, HALF), :].astype(F32)
                            if w == 0:
                                early[q * NF + g, pl.ds(at, HALF), :] = total
                            else:
                                late[q * NF + g, pl.ds(at + 2 * LAGMAX, HALF), :] = total

        def wrap(k, inner):
            late[k, pl.ds(0, 2 * LAGMAX), :] = pltpu.roll(late[k, pl.ds(XS, 2 * LAGMAX), :], ROWS, 1)
            late[k, pl.ds(XS + 2 * LAGMAX, 2 * LAGMAX), :] = pltpu.roll(
                late[k, pl.ds(2 * LAGMAX, 2 * LAGMAX), :], XS - ROWS, 1
            )
            return inner

        lax.fori_loop(0, batch, wrap, 0)

        def tile(i, inner):
            at = pl.multiple_of(i * HALF, HALF)
            starts = [at + offset for offset in offsets]

            def add(k, totals):
                for step in range(4):
                    one = early[4 * k + step, pl.ds(at, HALF), :]
                    totals = tuple(
                        total + one * late[4 * k + step, pl.ds(start, HALF), :]
                        for total, start in zip(totals, starts)
                    )
                return totals

            totals = lax.fori_loop(
                0, batch // 4, add, tuple(sums[h, pl.ds(at + LAGMAX, HALF), :] for h in range(lags))
            )
            for h in range(lags):
                sums[h, pl.ds(at + LAGMAX, HALF), :] = totals[h]
            return inner

        return lax.fori_loop(0, XS // HALF, tile, carry)

    lax.fori_loop(0, TERMS // ROUND, one_round, 0)

    x = (
        lax.broadcasted_iota(jnp.int32, (XS, XS), 0)
        + lax.broadcasted_iota(jnp.int32, (XS, XS), 1) // ROWS * XS
    )
    weight = 1.0 / (STEPS * terms / 2)

    def finish(h, carry):
        lag = lag_ref[h]
        sums[h, pl.ds(0, LAGMAX), :] = pltpu.roll(sums[h, pl.ds(XS, LAGMAX), :], ROWS, 1)
        sums[h, pl.ds(XS + LAGMAX, LAGMAX), :] = pltpu.roll(sums[h, pl.ds(LAGMAX, LAGMAX), :], XS - ROWS, 1)
        moved = sums[h, pl.ds(LAGMAX - lag, XS), :]
        reach = jnp.abs(lag)
        kept = jnp.where((x >= reach) & (x < COLS - reach), moved * weight, 0.0).T
        for c in range(BLOCKS):
            out[h, :, pl.ds(XS * c, XS)] = kept[ROWS * c : ROWS * (c + 1)].astype(BF16)
        return carry

    lax.fori_loop(0, lags, finish, 0)

    def sent(r, carry):
        for present, up, down in sides:
            @pl.when(present)
            def _(up=up, down=down):
                halo_copy(r, up, down).wait_send()

        return carry

    lax.fori_loop(0, ROUNDS, sent, 0)

    for present, up, down in sides[:4]:
        @pl.when(present)
        def _(up=up, down=down):
            first_copy(up, down).wait_send()

    def spectra_sent(k, carry):
        for o in range(NF - 1):
            spec_copy(o, k).wait_send()
        return carry

    lax.fori_loop(0, TERMS, spectra_sent, 0)

    def delivered(batch, carry):
        for n in range(4):
            @pl.when(jnp.logical_not(owns & (post == n)))
            def _(n=n):
                held_copy(n, batch).wait_send()

        return carry

    lax.fori_loop(0, STEPS // 4, delivered, 0)

    for n in range(4):
        @pl.when(home != n)
        def _(n=n):
            relay_copy(n).wait_send()

        @pl.when(jnp.logical_not(mine & (f == n)))
        def _(n=n):
            piece_copy(n).wait_send()


def body(
    previous_field, current_field, courant, wavelet, traces, source_cell, receiver_cells,
    frequency_list, lag_list, spectra,
):
    lags, terms = lag_list.shape[0], NF * TERMS
    table = dft_table(frequency_list).reshape(STEPS, NF, TERMS).transpose(2, 1, 0).reshape(terms, STEPS)
    vmem = pl.BlockSpec(memory_space=pltpu.VMEM)
    smem = pl.BlockSpec(memory_space=pltpu.SMEM)
    dma = pltpu.SemaphoreType.DMA
    pair = (2 * WIDE, COLS)
    image = pl.pallas_call(
        kernel,
        out_shape=jax.ShapeDtypeStruct((lags, ROWS, COLS), BF16),
        in_specs=[vmem, vmem, vmem, smem, vmem, smem, vmem, smem, vmem, pl.BlockSpec(memory_space=pl.ANY)],
        out_specs=vmem,
        scratch_shapes=[
            pltpu.VMEM((NF, 2, TERMS, ROWS, COLS), F32),
            pltpu.VMEM((NF - 1, TERMS, 2, XS, XS), BF16),
            pltpu.VMEM((NF, TERMS, 2, XS, XS), BF16),
            pltpu.VMEM((4, 6, DEEP * WIDE, 128), BF16),
            pltpu.VMEM((4, 6, DEEP * WIDE, 128), BF16),
            pltpu.VMEM((NF, 6, DEEP * WIDE, 128), BF16),
            pltpu.VMEM((2, DEEP + 4, 2, RING, COLS), F32),
            pltpu.VMEM((DEEP + 2, RING, COLS), F32),
            pltpu.VMEM((STEPS, DEEP + 2, RING, COLS), F32),
            pltpu.VMEM((STEPS + 1, DEEP) + pair, BF16),
            pltpu.VMEM((STEPS, 4) + pair, BF16),
            pltpu.VMEM((ROUNDS, 2) + pair, BF16),
            pltpu.VMEM((ROUNDS, 2) + pair, BF16),
            pltpu.VMEM((ROUNDS, 2, 4 * DEEP, COLS), BF16),
            pltpu.VMEM((ROUNDS, 2, 4 * DEEP, COLS), BF16),
            pltpu.VMEM((ROUNDS, 2, 2, 8, 128), F32),
            pltpu.VMEM((ROUNDS, 2, 2, 8, 128), F32),
            pltpu.VMEM((2, 3, WIDE, COLS), F32),
            pltpu.VMEM((2, 4 * DEEP, COLS), F32),
            pltpu.VMEM((3, WIDE, COLS), F32),
            pltpu.VMEM((3, WIDE, COLS), F32),
            pltpu.VMEM((2, 4 * DEEP, COLS), F32),
            pltpu.VMEM((terms, STEPS * HALF), F32),
            pltpu.VMEM((terms * HALF, STEPS * HALF), BF16),
            pltpu.VMEM((2, XS // HALF // 2, STEPS, HALF, 2 * XS), BF16),
            pltpu.VMEM((ROUND * NF, XS, XS), F32),
            pltpu.VMEM((ROUND * NF, XS + 4 * LAGMAX, XS), F32),
            pltpu.VMEM((lags, XS + 2 * LAGMAX, XS), F32),
            dma((NF, 2)),
            dma((NF - 1, TERMS)),
            dma((NF, TERMS)),
            dma((4,)),
            dma((4,)),
            dma((4,)),
            dma((NF,)),
            dma((ROUNDS, 2)),
            dma((ROUNDS, 2)),
            dma((ROUNDS, 2)),
            dma((ROUNDS, 2)),
            dma((ROUNDS, 4)),
            dma((ROUNDS, 4)),
            dma((4,)),
            dma((4,)),
            dma((STEPS // 4, 4)),
            dma((STEPS // 4, 4)),
        ],
        compiler_params=pltpu.CompilerParams(
            collective_id=0, has_side_effects=True, vmem_limit_bytes=56 * 2**20
        ),
        name="window_image",
    )(
        previous_field, current_field, courant, wavelet, traces, source_cell,
        receiver_cells.reshape(1, -1), lag_list, table, spectra.reshape(2, TERMS, NY, COLS),
    )
    return image.reshape(lags, 1, 1, ROWS, COLS)


def solution(mesh):
    placed = (
        P(None, "xy", "slab", "freq"),
        P(None, "xy", "slab", "freq"),
        P("xy", "slab", "freq"),
        P(),
        P(),
        P(),
        P(),
        P(),
        P(),
        P(None, "freq", None, "xy", "slab", None, None),
    )
    return jax.shard_map(
        body,
        mesh=mesh,
        in_specs=placed,
        out_specs=P(None, "xy", "slab", "freq", None),
        check_vma=False,
    )
```

```python
import math

import jax
import jax.numpy as jnp
from jax import lax
from jax.experimental import pallas as pl
from jax.experimental.pallas import tpu as pltpu
from jax.sharding import PartitionSpec as P

STEPS = 16
NTOT = 2048
LAGMAX = 16
NF, NS, NB = 4, 16, 4
ROWS, COLS = 32, 512
DEEP, WIDE = 4, 8
RING = 16
TERMS = 16
NY = NF * ROWS
F32, BF16 = jnp.float32, jnp.bfloat16
XS = 128
BLOCKS = COLS // XS
HALF = 16
ROUND = 2
ROUNDS = STEPS // 2
AHEAD, EACH, BESIDE = 1, 1, 9
MESH = pl.DeviceIdType.MESH


def dft_table(frequency_list):
    moments = jnp.arange(STEPS, dtype=jnp.int32) + (NTOT - STEPS)
    phase_index = moments[:, None] * frequency_list[None, :] % NTOT
    phase_angle = phase_index.astype(F32) * (2.0 * math.pi / NTOT)
    return jnp.stack([jnp.cos(phase_angle), -jnp.sin(phase_angle)], axis=-1).astype(BF16)


def swung(outer, inner):
    return inner + outer % 2 * (3 - 2 * inner)


def turned(rows):
    return jnp.concatenate([rows[:, XS * c : XS * (c + 1)] for c in range(BLOCKS)], axis=0).T


def kernel(
    prev_ref, cur_ref, cour_ref, wav_ref, traces_ref, src_ref, rec_ref, lag_ref, table_ref, spec_ref,
    out,
    raw, outgoing, fresh, pieces_out, relay, pieces_in, field, cour, inj, planes, held, lo, hi, yout, yin, corner_out, corner, first_z, first_y, first_lo, first_hi, first_in,
    spread, mix, snaps, early, late, sums,
    raw_sem, spec_send, spec_recv, relay_send, relay_recv, piece_send, piece_recv,
    zsend, zrecv, ysend, yrecv, csend, crecv, fsend, frecv, held_send, held_recv,
):
    f, j, b = lax.axis_index("freq"), lax.axis_index("slab"), lax.axis_index("xy")
    home, post = j // 4, j % 4
    deep, wide = swung(b, home), swung(f, post)
    layer, strip = b * 4 + deep, f * 4 + wide
    first_plane, first_row = layer * DEEP, strip * WIDE
    has_lo, has_hi = layer > 0, layer < NB * 4 - 1
    has_top, has_bottom = strip > 0, strip < NF * 4 - 1
    lags = lag_ref.shape[0]

    def block_at(up, down):
        to_layer, to_strip = layer + up, strip + down
        return {
            "freq": to_strip // 4,
            "slab": swung(to_layer // 4, to_layer % 4) * 4 + swung(to_strip // 4, to_strip % 4),
            "xy": to_layer // 4,
        }

    def group_at(other):
        return {"freq": other, "slab": j, "xy": b}

    def plane_at(other):
        return {"freq": f, "slab": deep * 4 + other, "xy": b}

    peers = (lax.rem(f + 2, NF), NF - 1 - f, f + 1 - 2 * lax.rem(f, 2))
    chunk = peers + (f,)
    owns = b % 2 == 0

    def raw_copy(o, w):
        return pltpu.make_async_copy(
            spec_ref.at[w, :, pl.ds(chunk[o] * ROWS, ROWS), :], raw.at[o, w], raw_sem.at[o, w]
        )

    for o in range(NF):
        for w in range(2):
            raw_copy(o, w).start()

    barrier = pltpu.get_barrier_semaphore()
    mine = f % 2 == 0

    def greet(there):
        pl.semaphore_signal(barrier, 1, device_id=there, device_id_type=MESH)

    for p in peers:
        greet(group_at(p))
    for n in range(4):
        @pl.when(jnp.logical_not(owns & (post == n)))
        def _(n=n):
            greet(plane_at(n))

    sides = (
        (has_hi, 1, 0), (has_lo, -1, 0), (has_bottom, 0, 1), (has_top, 0, -1),
        (has_hi & has_bottom, 1, 1), (has_hi & has_top, 1, -1),
        (has_lo & has_bottom, -1, 1), (has_lo & has_top, -1, -1),
    )
    for present, up, down in sides:
        @pl.when(present)
        def _(up=up, down=down):
            greet(block_at(up, down))

    for n in range(4):
        @pl.when(home != n)
        def _(n=n):
            greet({"freq": f, "slab": 4 * n + post, "xy": b})

    for f0 in range(NF):
        @pl.when(jnp.logical_not(mine & (f == f0)))
        def _(f0=f0):
            greet({"freq": f0, "slab": 4 * home + wide, "xy": b})

    def stack(group, carry):
        at = pl.ds(group * DEEP, DEEP)
        for w in range(2):
            pieces_out[group, w] = prev_ref[w, at].reshape(DEEP * WIDE, 128).astype(BF16)
            pieces_out[group, 2 + w] = cur_ref[w, at].reshape(DEEP * WIDE, 128).astype(BF16)
        exact = cour_ref[at].reshape(DEEP * WIDE, 128)
        rounded = exact.astype(BF16)
        pieces_out[group, 4] = rounded
        pieces_out[group, 5] = (exact - rounded.astype(F32)).astype(BF16)
        return carry

    lax.fori_loop(0, 4, stack, 0)

    expected = len(peers) + 4 + 3 + NF - mine.astype(jnp.int32) - owns.astype(jnp.int32)
    for present, _, _ in sides:
        expected += present.astype(jnp.int32)
    pl.semaphore_wait(barrier, expected)

    def relay_copy(n):
        group = swung(b, n)
        return pltpu.make_async_remote_copy(
            src_ref=pieces_out.at[group],
            dst_ref=relay.at[home],
            send_sem=relay_send.at[n],
            recv_sem=relay_recv.at[home],
            device_id={"freq": f, "slab": 4 * n + post, "xy": b},
            device_id_type=MESH,
        )

    def piece_copy(n):
        return pltpu.make_async_remote_copy(
            src_ref=relay.at[n],
            dst_ref=pieces_in.at[f],
            send_sem=piece_send.at[n],
            recv_sem=piece_recv.at[f],
            device_id={"freq": n, "slab": 4 * home + swung(n, post), "xy": b},
            device_id_type=MESH,
        )

    for n in range(4):
        @pl.when(home != n)
        def _(n=n):
            relay_copy(n).start()

    relay[home] = pieces_out[deep]

    for n in range(4):
        @pl.when(home != n)
        def _(n=n):
            pltpu.make_async_remote_copy(
                src_ref=pieces_out.at[n], dst_ref=relay.at[n],
                send_sem=relay_send.at[n], recv_sem=relay_recv.at[n],
                device_id={"freq": f, "slab": 4 * n + post, "xy": b}, device_id_type=MESH,
            ).wait_recv()

        @pl.when(jnp.logical_not(mine & (f == n)))
        def _(n=n):
            piece_copy(n).start()

    @pl.when(mine)
    def _():
        pieces_in[f] = relay[f]

    def spec_copy(o, k):
        return pltpu.make_async_remote_copy(
            src_ref=outgoing.at[o, k],
            dst_ref=fresh.at[f, k],
            send_sem=spec_send.at[o, k],
            recv_sem=spec_recv.at[f, k],
            device_id=group_at(peers[o]),
            device_id_type=MESH,
        )

    def send_spectra(k):
        for o in range(NF - 1):
            for w in range(2):
                outgoing[o, k, w] = turned(raw[o, w, k]).astype(BF16)
            spec_copy(o, k).start()
        for w in range(2):
            fresh[f, k, w] = turned(raw[NF - 1, w, k]).astype(BF16)

    for o in range(NF):
        for w in range(2):
            raw_copy(o, w).wait()

    for k in range(AHEAD):
        send_spectra(k)

    cell = rec_ref[...]
    depth, row, col = (cell >> 16) - first_plane + 1, ((cell >> 9) & (NY - 1)) - first_row, cell & (COLS - 1)
    here = (depth >= 0) & (depth < DEEP + 2) & (row >= -1) & (row <= WIDE)
    row = jnp.where(here, depth * RING + (row & (RING - 1)), -1)
    size = (DEEP + 2) * RING
    at_row = lax.broadcasted_iota(jnp.int32, (size, cell.shape[1]), 0) == row
    at_col = (lax.broadcasted_iota(jnp.int32, (COLS, cell.shape[1]), 0) == col).astype(F32).astype(BF16)

    def inject(t, carry):
        values = jnp.where(at_row, traces_ref[pl.ds(t, 1), :], 0.0)
        first = values.astype(BF16)
        rest = values - first.astype(F32)
        second = rest.astype(BF16)
        third = (rest - second.astype(F32)).astype(BF16)
        parts = lax.dot_general(
            jnp.concatenate([first, second, third], axis=0), at_col,
            (((1,), (1,)), ((), ())), preferred_element_type=F32,
        )
        total = parts[:size] + parts[size : 2 * size] + parts[2 * size :]
        inj[t] = total.reshape(DEEP + 2, RING, COLS)
        return carry

    terms = NF * TERMS
    step_of = lax.broadcasted_iota(jnp.int32, (STEPS, STEPS * HALF), 1) // HALF
    chosen = (step_of == lax.broadcasted_iota(jnp.int32, (STEPS, STEPS * HALF), 0)).astype(F32).astype(BF16)
    spread[...] = jnp.dot(table_ref[...], chosen, preferred_element_type=F32)
    place = lax.broadcasted_iota(jnp.int32, (HALF, STEPS * HALF), 1) % HALF
    diagonal = place == lax.broadcasted_iota(jnp.int32, (HALF, STEPS * HALF), 0)

    def fill(k, carry):
        values = jnp.where(diagonal, spread[pl.ds(k, 1), :], 0.0)
        mix[pl.ds(pl.multiple_of(k * HALF, HALF), HALF), :] = values.astype(BF16)
        return carry

    def clear_plane(p, carry):
        for n in range(2):
            for w in range(2):
                field[n, p, w] = jnp.zeros((RING, COLS), F32)

        @pl.when(p < DEEP + 2)
        def _():
            cour[p] = jnp.zeros((RING, COLS), F32)

        return carry

    lax.fori_loop(0, DEEP + 4, clear_plane, 0)

    for f0 in range(NF):
        @pl.when(jnp.logical_not(mine & (f == f0)))
        def _(f0=f0):
            pltpu.make_async_remote_copy(
                src_ref=pieces_out.at[0], dst_ref=pieces_in.at[f0],
                send_sem=piece_send.at[0], recv_sem=piece_recv.at[f0],
                device_id=group_at(f), device_id_type=MESH,
            ).wait_recv()

        cols = pl.ds(128 * f0, 128)
        piece = [pieces_in[f0, n].astype(F32) for n in range(6)]
        for p in range(DEEP):
            rows = slice(WIDE * p, WIDE * (p + 1))
            for w in range(2):
                field[1, p + 2, w, pl.ds(0, WIDE), cols] = piece[w][rows]
                field[0, p + 2, w, pl.ds(0, WIDE), cols] = piece[2 + w][rows]
            cour[p + 1, pl.ds(0, WIDE), cols] = piece[4][rows] + piece[5][rows]

    def halo_copy(r, up, down):
        if not down:
            low = up > 0
            src, dst = planes.at[2 * r, pl.ds(DEEP - 2 if low else 0, 2)], (lo if low else hi).at[r]
            sems = zsend.at[r, int(low)], zrecv.at[r, int(low)]
        elif not up:
            n = int(down > 0)
            src, dst, sems = yout.at[r, n], yin.at[r, n], (ysend.at[r, n], yrecv.at[r, n])
        else:
            n, m = int(down > 0), int(up > 0)
            src, dst = corner_out.at[r, m, n], corner.at[r, m, n]
            sems = csend.at[r, 2 * m + n], crecv.at[r, 2 * m + n]
        return pltpu.make_async_remote_copy(
            src_ref=src, dst_ref=dst, send_sem=sems[0], recv_sem=sems[1],
            device_id=block_at(up, down), device_id_type=MESH,
        )

    def first_copy(up, down):
        n = int(up + down > 0)
        if up:
            src, dst, m = first_z.at[n], (first_lo if n else first_hi), n
        else:
            src, dst, m = first_y.at[n], first_in.at[n], 2 + n
        return pltpu.make_async_remote_copy(
            src_ref=src, dst_ref=dst, send_sem=fsend.at[m], recv_sem=frecv.at[m],
            device_id=block_at(up, down), device_id_type=MESH,
        )

    def publish(s, p, values):
        planes[s, p] = jnp.concatenate(values, axis=0).astype(BF16)

    def send(r, values):
        for n, at in ((0, 0), (1, WIDE - 2)):
            rows = [values[p][w][at : at + 2] for p in range(DEEP) for w in range(2)]
            yout[r, n] = jnp.concatenate(rows, axis=0).astype(BF16)
        for m, p in ((0, 0), (1, DEEP - 1)):
            for n, at in ((0, 0), (1, WIDE - 1)):
                rows = [
                    values[p][w][at : at + 1, 128 * c : 128 * (c + 1)] for w in range(2) for c in range(4)
                ]
                corner_out[r, m, n] = jnp.concatenate(rows, axis=0)
        for present, up, down in sides[2:] + sides[:2]:
            @pl.when(present)
            def _(up=up, down=down):
                halo_copy(r, up, down).start()

    def held_copy(n, batch):
        return pltpu.make_async_remote_copy(
            src_ref=planes.at[pl.ds(4 * batch + 1, 4), n],
            dst_ref=held.at[pl.ds(4 * batch, 4), wide],
            send_sem=held_send.at[batch, n],
            recv_sem=held_recv.at[batch, wide],
            device_id=plane_at(n),
            device_id_type=MESH,
        )

    initial = [[field[0, p + 2, w, pl.ds(0, WIDE), :] for w in range(2)] for p in range(DEEP)]
    for p in range(DEEP):
        publish(0, p, initial[p])
    send(0, initial)

    for n, p, row in ((0, 0, 0), (1, DEEP - 1, WIDE - 1)):
        for w in range(2):
            first_z[n, w] = field[1, p + 2, w, pl.ds(0, WIDE), :]
            for q in range(DEEP):
                first_y[n, pl.ds(DEEP * w + q, 1), :] = field[1, q + 2, w, pl.ds(row, 1), :]
        first_z[n, 2] = cour[p + 1, pl.ds(0, WIDE), :]
        for q in range(DEEP):
            first_y[n, pl.ds(2 * DEEP + q, 1), :] = cour[q + 1, pl.ds(row, 1), :]
        first_y[n, pl.ds(3 * DEEP, DEEP), :] = jnp.zeros((DEEP, COLS), F32)
    for present, up, down in sides[:4]:
        @pl.when(present)
        def _(up=up, down=down):
            first_copy(up, down).start()

    for present, up, down in sides[:4]:
        @pl.when(present)
        def _(up=up, down=down):
            first_copy(-up, -down).wait_recv()
            if up:
                there, at = (first_hi, DEEP + 2) if up > 0 else (first_lo, 1)
                for w in range(2):
                    field[1, at, w, pl.ds(0, WIDE), :] = there[w]
                cour[at - 1, pl.ds(0, WIDE), :] = there[2]
            else:
                n, at = (0, WIDE) if down > 0 else (1, RING - 1)
                for q in range(DEEP):
                    for w in range(2):
                        field[1, q + 2, w, pl.ds(at, 1), :] = first_in[n, pl.ds(DEEP * w + q, 1), :]
                    cour[q + 1, pl.ds(at, 1), :] = first_in[n, pl.ds(2 * DEEP + q, 1), :]

    row_id = lax.broadcasted_iota(jnp.int32, (RING, COLS), 0)
    col_id = lax.broadcasted_iota(jnp.int32, (RING, COLS), 1)
    source = src_ref[0]
    source_row = ((source >> 9) & (NY - 1)) - first_row
    source_row = jnp.where((source_row >= -1) & (source_row <= WIDE), source_row & (RING - 1), -1)
    source_plane = (source >> 16) - first_plane + 2
    at_source = (row_id == source_row) & (col_id == (source & (COLS - 1)))

    def step(t, now, p, w, height):
        u = field[now, p, w]
        beside = pltpu.roll(u, 1, 0)[:height] + pltpu.roll(u, RING - 1, 0)[:height]
        u = u[:height]
        beside += field[now, p - 1, w, pl.ds(0, height), :] + field[now, p + 1, w, pl.ds(0, height), :]
        col = col_id[:height]
        beside += jnp.where(col == 0, 0.0, pltpu.roll(u, 1, 1))
        beside += jnp.where(col == COLS - 1, 0.0, pltpu.roll(u, COLS - 1, 1))
        if w == 1:
            injection = inj[t, p - 1, pl.ds(0, height), :]
        else:
            injection = jnp.where(at_source[:height] & (source_plane == p), wav_ref[t], 0.0)
        before = field[1 - now, p, w, pl.ds(0, height), :]
        following = 2.0 * u - before + cour[p - 1, pl.ds(0, height), :] * (beside - 6.0 * u) + injection
        field[1 - now, p, w, pl.ds(0, height), :] = following
        return following

    def advance(r, carry):
        for i in range(EACH):
            k = AHEAD + EACH * r + i

            @pl.when(k < BESIDE)
            def _(k=k):
                send_spectra(k)

        lax.fori_loop(2 * r, 2 * r + 2, inject, 0)
        share = terms // ROUNDS
        lax.fori_loop(share * r, share * (r + 1), fill, 0)

        for present, up, down in sides:
            @pl.when(present)
            def _(up=up, down=down):
                halo_copy(r, -up, -down).wait_recv()
                if not down:
                    there, at = (hi, DEEP + 2) if up > 0 else (lo, 0)
                    for q in range(2):
                        both = there[r, q].astype(F32)
                        for w in range(2):
                            field[0, at + q, w, pl.ds(0, WIDE), :] = both[WIDE * w : WIDE * (w + 1)]
                    return
                n, at = (0, WIDE) if down > 0 else (1, RING - 2)
                if not up:
                    rows = yin[r, n].astype(F32)
                    for p in range(DEEP):
                        for w in range(2):
                            i = 4 * p + 2 * w
                            field[0, p + 2, w, pl.ds(at, 2), :] = rows[i : i + 2]
                else:
                    m, q = (0, DEEP + 2) if up > 0 else (1, 1)
                    at = WIDE if down > 0 else RING - 1
                    for w in range(2):
                        for c in range(4):
                            field[0, q, w, pl.ds(at, 1), pl.ds(128 * c, 128)] = corner[
                                r, m, n, pl.ds(4 * w + c, 1), :
                            ]

        t = 2 * r
        middle = [
            [step(t, 0, p, w, RING if 1 < p < DEEP + 2 else WIDE) for w in range(2)]
            for p in range(1, DEEP + 3)
        ]
        last = [[step(t + 1, 1, p, w, WIDE) for w in range(2)] for p in range(2, DEEP + 2)]
        for p in range(DEEP):
            publish(t + 2, p, last[p])

        @pl.when(r < ROUNDS - 1)
        def _():
            send(r + 1, last)

        for p in range(DEEP):
            publish(t + 1, p, [values[:WIDE] for values in middle[p + 1]])

        @pl.when(owns)
        def _():
            for i in (1, 2):
                held[t + i - 1, wide] = planes[t + i, post]

        for n in range(4):
            @pl.when((r % 2 == 1) & jnp.logical_not(owns & (post == n)))
            def _(n=n):
                held_copy(n, r // 2).start()

        return carry

    lax.fori_loop(0, ROUNDS, advance, 0)

    def rest(k, carry):
        send_spectra(k)
        return carry

    lax.fori_loop(BESIDE, TERMS, rest, 0)

    def turn_batch(batch, carry):
        for n in range(4):
            @pl.when(jnp.logical_not(owns & (post == n)))
            def _(n=n):
                pltpu.make_async_remote_copy(
                    src_ref=planes.at[pl.ds(4 * batch + 1, 4), n],
                    dst_ref=held.at[pl.ds(4 * batch, 4), swung(f, n)],
                    send_sem=held_send.at[batch, n], recv_sem=held_recv.at[batch, swung(f, n)],
                    device_id=plane_at(n), device_id_type=MESH,
                ).wait_recv()

        def turn(q, inner):
            t = 4 * batch + q
            strips = held[t].astype(F32)
            for w in range(2):
                plane = turned(strips[:, WIDE * w : WIDE * (w + 1)].reshape(ROWS, COLS)).astype(BF16)
                for i in range(XS // HALF):
                    snaps[w, i // 2, t, :, pl.ds((i % 2) * XS, XS)] = plane[HALF * i : HALF * (i + 1)]
            return inner

        return lax.fori_loop(0, 4, turn, carry)

    lax.fori_loop(0, STEPS // 4, turn_batch, 0)

    offsets = [2 * lag_ref[h] + 2 * LAGMAX for h in range(lags)]
    batch = ROUND * NF

    def clear(h, carry):
        sums[h] = jnp.zeros(sums.shape[1:], F32)
        return carry

    lax.fori_loop(0, lags, clear, 0)

    def one_round(r, carry):
        def arrive(q, inner):
            k = r * ROUND + q
            for o in range(NF - 1):
                pltpu.make_async_remote_copy(
                    src_ref=outgoing.at[o, k], dst_ref=fresh.at[peers[o], k],
                    send_sem=spec_send.at[o, k], recv_sem=spec_recv.at[peers[o], k],
                    device_id=group_at(peers[o]), device_id_type=MESH,
                ).wait_recv()
            return inner

        lax.fori_loop(0, ROUND, arrive, 0)
        size = batch * HALF
        table = mix[pl.ds(pl.multiple_of(r * size, size), size), :]
        for w in range(2):
            for pair in range(XS // HALF // 2):
                moments = snaps[w, pair].reshape(STEPS * HALF, 2 * XS)
                part = jnp.dot(table, moments, preferred_element_type=F32).reshape(batch, HALF, 2 * XS)
                for q in range(ROUND):
                    for g in range(NF):
                        for i in range(2):
                            at = HALF * (2 * pair + i)
                            total = part[q * NF + g, :, XS * i : XS * (i + 1)]
                            total += fresh[g, r * ROUND + q, w, pl.ds(at, HALF), :].astype(F32)
                            if w == 0:
                                early[q * NF + g, pl.ds(at, HALF), :] = total
                            else:
                                late[q * NF + g, pl.ds(at + 2 * LAGMAX, HALF), :] = total

        def wrap(k, inner):
            late[k, pl.ds(0, 2 * LAGMAX), :] = pltpu.roll(late[k, pl.ds(XS, 2 * LAGMAX), :], ROWS, 1)
            late[k, pl.ds(XS + 2 * LAGMAX, 2 * LAGMAX), :] = pltpu.roll(
                late[k, pl.ds(2 * LAGMAX, 2 * LAGMAX), :], XS - ROWS, 1
            )
            return inner

        lax.fori_loop(0, batch, wrap, 0)

        def tile(i, inner):
            at = pl.multiple_of(i * HALF, HALF)
            starts = [at + offset for offset in offsets]

            def add(k, totals):
                for step in range(4):
                    one = early[4 * k + step, pl.ds(at, HALF), :]
                    totals = tuple(
                        total + one * late[4 * k + step, pl.ds(start, HALF), :]
                        for total, start in zip(totals, starts)
                    )
                return totals

            totals = lax.fori_loop(
                0, batch // 4, add, tuple(sums[h, pl.ds(at + LAGMAX, HALF), :] for h in range(lags))
            )
            for h in range(lags):
                sums[h, pl.ds(at + LAGMAX, HALF), :] = totals[h]
            return inner

        return lax.fori_loop(0, XS // HALF, tile, carry)

    lax.fori_loop(0, TERMS // ROUND, one_round, 0)

    x = (
        lax.broadcasted_iota(jnp.int32, (XS, XS), 0)
        + lax.broadcasted_iota(jnp.int32, (XS, XS), 1) // ROWS * XS
    )
    weight = 1.0 / (STEPS * terms / 2)

    def finish(h, carry):
        lag = lag_ref[h]
        sums[h, pl.ds(0, LAGMAX), :] = pltpu.roll(sums[h, pl.ds(XS, LAGMAX), :], ROWS, 1)
        sums[h, pl.ds(XS + LAGMAX, LAGMAX), :] = pltpu.roll(sums[h, pl.ds(LAGMAX, LAGMAX), :], XS - ROWS, 1)
        moved = sums[h, pl.ds(LAGMAX - lag, XS), :]
        reach = jnp.abs(lag)
        kept = jnp.where((x >= reach) & (x < COLS - reach), moved * weight, 0.0).T
        for c in range(BLOCKS):
            out[h, :, pl.ds(XS * c, XS)] = kept[ROWS * c : ROWS * (c + 1)].astype(BF16)
        return carry

    lax.fori_loop(0, lags, finish, 0)

    def sent(r, carry):
        for present, up, down in sides:
            @pl.when(present)
            def _(up=up, down=down):
                halo_copy(r, up, down).wait_send()

        return carry

    lax.fori_loop(0, ROUNDS, sent, 0)

    for present, up, down in sides[:4]:
        @pl.when(present)
        def _(up=up, down=down):
            first_copy(up, down).wait_send()

    def spectra_sent(k, carry):
        for o in range(NF - 1):
            spec_copy(o, k).wait_send()
        return carry

    lax.fori_loop(0, TERMS, spectra_sent, 0)

    def delivered(batch, carry):
        for n in range(4):
            @pl.when(jnp.logical_not(owns & (post == n)))
            def _(n=n):
                held_copy(n, batch).wait_send()

        return carry

    lax.fori_loop(0, STEPS // 4, delivered, 0)

    for n in range(4):
        @pl.when(home != n)
        def _(n=n):
            relay_copy(n).wait_send()

        @pl.when(jnp.logical_not(mine & (f == n)))
        def _(n=n):
            piece_copy(n).wait_send()


def body(
    previous_field, current_field, courant, wavelet, traces, source_cell, receiver_cells,
    frequency_list, lag_list, spectra,
):
    lags, terms = lag_list.shape[0], NF * TERMS
    table = dft_table(frequency_list).reshape(STEPS, NF, TERMS).transpose(2, 1, 0).reshape(terms, STEPS)
    vmem = pl.BlockSpec(memory_space=pltpu.VMEM)
    smem = pl.BlockSpec(memory_space=pltpu.SMEM)
    dma = pltpu.SemaphoreType.DMA
    pair = (2 * WIDE, COLS)
    image = pl.pallas_call(
        kernel,
        out_shape=jax.ShapeDtypeStruct((lags, ROWS, COLS), BF16),
        in_specs=[vmem, vmem, vmem, smem, vmem, smem, vmem, smem, vmem, pl.BlockSpec(memory_space=pl.ANY)],
        out_specs=vmem,
        scratch_shapes=[
            pltpu.VMEM((NF, 2, TERMS, ROWS, COLS), F32),
            pltpu.VMEM((NF - 1, TERMS, 2, XS, XS), BF16),
            pltpu.VMEM((NF, TERMS, 2, XS, XS), BF16),
            pltpu.VMEM((4, 6, DEEP * WIDE, 128), BF16),
            pltpu.VMEM((4, 6, DEEP * WIDE, 128), BF16),
            pltpu.VMEM((NF, 6, DEEP * WIDE, 128), BF16),
            pltpu.VMEM((2, DEEP + 4, 2, RING, COLS), F32),
            pltpu.VMEM((DEEP + 2, RING, COLS), F32),
            pltpu.VMEM((STEPS, DEEP + 2, RING, COLS), F32),
            pltpu.VMEM((STEPS + 1, DEEP) + pair, BF16),
            pltpu.VMEM((STEPS, 4) + pair, BF16),
            pltpu.VMEM((ROUNDS, 2) + pair, BF16),
            pltpu.VMEM((ROUNDS, 2) + pair, BF16),
            pltpu.VMEM((ROUNDS, 2, 4 * DEEP, COLS), BF16),
            pltpu.VMEM((ROUNDS, 2, 4 * DEEP, COLS), BF16),
            pltpu.VMEM((ROUNDS, 2, 2, 8, 128), F32),
            pltpu.VMEM((ROUNDS, 2, 2, 8, 128), F32),
            pltpu.VMEM((2, 3, WIDE, COLS), F32),
            pltpu.VMEM((2, 4 * DEEP, COLS), F32),
            pltpu.VMEM((3, WIDE, COLS), F32),
            pltpu.VMEM((3, WIDE, COLS), F32),
            pltpu.VMEM((2, 4 * DEEP, COLS), F32),
            pltpu.VMEM((terms, STEPS * HALF), F32),
            pltpu.VMEM((terms * HALF, STEPS * HALF), BF16),
            pltpu.VMEM((2, XS // HALF // 2, STEPS, HALF, 2 * XS), BF16),
            pltpu.VMEM((ROUND * NF, XS, XS), F32),
            pltpu.VMEM((ROUND * NF, XS + 4 * LAGMAX, XS), F32),
            pltpu.VMEM((lags, XS + 2 * LAGMAX, XS), F32),
            dma((NF, 2)),
            dma((NF - 1, TERMS)),
            dma((NF, TERMS)),
            dma((4,)),
            dma((4,)),
            dma((4,)),
            dma((NF,)),
            dma((ROUNDS, 2)),
            dma((ROUNDS, 2)),
            dma((ROUNDS, 2)),
            dma((ROUNDS, 2)),
            dma((ROUNDS, 4)),
            dma((ROUNDS, 4)),
            dma((4,)),
            dma((4,)),
            dma((STEPS // 4, 4)),
            dma((STEPS // 4, 4)),
        ],
        compiler_params=pltpu.CompilerParams(
            collective_id=0, has_side_effects=True, vmem_limit_bytes=56 * 2**20
        ),
        name="window_image",
    )(
        previous_field, current_field, courant, wavelet, traces, source_cell,
        receiver_cells.reshape(1, -1), lag_list, table, spectra.reshape(2, TERMS, NY, COLS),
    )
    return image.reshape(lags, 1, 1, ROWS, COLS)


def solution(mesh):
    placed = (
        P(None, "xy", "slab", "freq"),
        P(None, "xy", "slab", "freq"),
        P("xy", "slab", "freq"),
        P(),
        P(),
        P(),
        P(),
        P(),
        P(),
        P(None, "freq", None, "xy", "slab", None, None),
    )
    return jax.shard_map(
        body,
        mesh=mesh,
        in_specs=placed,
        out_specs=P(None, "xy", "slab", "freq", None),
        check_vma=False,
    )
```
